512 devices in a mesh: grp: 64 (over y, x, core), tp: 8 (over z).
Axes of the slice: x: 4, y: 8, z: 8, core: 2. Of those that a mesh axis runs over, the one named last changes fastest.
Arguments:
- prefill_q: bfloat16 [16384, 4096], P('grp', 'tp'), may hold values from -32 to 32
- prefill_k: bfloat16 [16384, 1024], P('grp', 'tp'), may hold values from -32 to 32
- prefill_v: bfloat16 [16384, 1024], P('grp', 'tp'), may hold values from -6 to 6
- span_offset: int32 [64], P('grp'), may hold values from 0 to 32512
- page_group: int32 [1024, 1], P('grp'), may hold values from 0 to 63; in each aligned block of 16 rows (0 to 15, 16 to 31, ...) at most 2 rows name the same one
- page_request: int32 [1024], P('grp'), may hold values from 0 to 3
- decode_q: bfloat16 [256, 4096], P('grp', 'tp'), may hold values from -24 to 24
- cache_k: bfloat16 [256, 512, 1024], P('grp', None, 'tp'), may hold values from -24 to 24
- cache_v: bfloat16 [256, 512, 1024], P('grp', None, 'tp'), may hold values from -6 to 6
- cache_len: int32 [256], P('grp'), may hold values from 2 to 512, as said below
- out_weight: bfloat16 [4096, 8192], P('tp', 'grp'), may hold values from -0.09375 to 0.09375
Outputs:
- prefill_out: bfloat16 [16384, 4096], P('grp', 'tp')
- decode_out: bfloat16 [256, 8192], P('tp', 'grp')
The draws below stay inside these ranges and needn't reach their ends.
Inputs may be any that keep to these rules, and one draw needn't show every extreme that they name: `page_group`: among the 16 pages of one span no group is named by more than 2 pages, and some span names one group exactly 2 times. `cache_len`: some request has exactly 512 live slots.
All inputs are finite; a program needn't handle non-finite values.
Results may differ from the reference program's by a relative error of at most 0.014.
Values may be sent and summed in bfloat16 or wider, within the bound.
No kernel may reach another device: no remote copies, remote signals or barrier semaphores. Data moves between devices by JAX's collectives and lax.ppermute only.
A program may use at most 64 MiB of HBM per device.

```python
import math
import jax
import jax.numpy as jnp
import numpy as np
from jax import lax

D = 8192
HD = 128
KVH = 8
QPK = 4
QH = 32
CH = 256
PAGE = 16
PCH = 16
CAP = 2
REQ = 4
REQUESTS = 256
LRES = 512
N_GRP = 64


def draw_prefill_q(key, part):
    key = jax.random.fold_in(key, 1)
    shape_full = (N_GRP * CH, KVH, QPK, HD)
    drawn = jnp.clip(jax.random.normal(key, shape_full, jnp.float32), -6.0, 6.0)
    return drawn.reshape(N_GRP * CH, QH * HD).astype(jnp.bfloat16)


def draw_prefill_k(key, part):
    key = jax.random.fold_in(key, 2)
    shape_full = (N_GRP * CH, KVH, HD)
    drawn = jnp.clip(jax.random.normal(key, shape_full, jnp.float32), -6.0, 6.0)
    return drawn.reshape(N_GRP * CH, KVH * HD).astype(jnp.bfloat16)


def draw_decode_q(key, part):
    key = jax.random.fold_in(key, 3)
    shape_full = (REQUESTS, KVH, QPK, HD)
    drawn = jnp.clip(jax.random.normal(key, shape_full, jnp.float32), -6.0, 6.0)
    return drawn.reshape(REQUESTS, QH * HD).astype(jnp.bfloat16)


def draw_cache_k(key, part):
    key = jax.random.fold_in(key, 4)
    shape_full = (REQUESTS, LRES, KVH, HD)
    drawn = jnp.clip(jax.random.normal(key, shape_full, jnp.float32), -6.0, 6.0)
    return drawn.reshape(REQUESTS, LRES, KVH * HD).astype(jnp.bfloat16)


def draw_cache_len(key, part):
    key = jax.random.fold_in(key, 7)
    lengths = jax.random.randint(key, (REQUESTS,), 2, LRES + 1)
    full_place = jax.random.randint(jax.random.fold_in(key, 8), (), 0, REQUESTS)
    return jnp.where(jnp.arange(REQUESTS) == full_place, LRES, lengths).astype(jnp.int32)


def plant(values, stream_key, least, high):
    longest = values.shape.index(max(values.shape))
    spots = []
    for shift in (0, 1):
        where = [jax.random.randint(jax.random.fold_in(stream_key, axis), (), 0, length) for axis, length in enumerate(values.shape)]
        where[longest] = (where[longest] + shift) % values.shape[longest]
        spots.append(tuple(where))
    return values.at[spots[0]].set(least).at[spots[1]].set(high)


def block_levels(own_key, dims, cuts, low, high):
    def one(position, blocks):
        steps = jax.random.uniform(jax.random.fold_in(jax.random.fold_in(own_key, 6), position), (blocks,), jnp.float32, low / len(cuts), high / len(cuts))
        return jnp.repeat(jnp.exp(steps), dims[position] // blocks).reshape((-1,) + (1,) * (len(dims) - position - 1))

    level = one(*cuts[0])
    for cut in cuts[1:]:
        level = level * one(*cut)
    return level


def deal_out(stream_key, own, number, rows, number_of, top, most, lean):
    sequence = jax.random.permutation(stream_key, number_of)
    crowded, usual = shares(number_of, rows * top, most, lean, True), shares(number_of, rows * top, most, lean, False)
    places = jnp.arange(number_of)

    def named(tallies, turn):
        used = int((tallies > 0).sum())
        fixed = max(1, used // 4)
        shifted = fixed + (places - fixed + turn * (used - fixed)) % max(1, number_of - fixed)
        return jnp.zeros((number_of,), jnp.int32).at[sequence[jnp.where(places < fixed, places, shifted)]].set(jnp.asarray(tallies, jnp.int32))

    tallies = jnp.where(number % 4 == 0, named(crowded, number // 4), named(usual, number - number // 4 - 1))
    mixed = jax.random.permutation(jax.random.fold_in(own, 3), number_of)
    source_of, sink = mixed[0:number_of // 2 * 2:2], mixed[1:number_of // 2 * 2:2]
    slack = jnp.minimum(tallies[source_of] - 1, most - tallies[sink]) // 2
    slack = jnp.where((source_of == sequence[0]) | (sink == sequence[0]) | (tallies[sink] == 0), 0, jnp.maximum(slack, 0))
    shifted = jax.random.randint(jax.random.fold_in(own, 4), (number_of // 2,), 0, 1 << 20) % (slack + 1)
    tallies = tallies.at[source_of].add(-shifted).at[sink].add(shifted)
    items = jnp.searchsorted(jnp.cumsum(tallies), jnp.arange(rows * top), side="right").astype(jnp.int32)
    listing = items.reshape(top, rows).T
    listing = listing[jax.random.permutation(jax.random.fold_in(own, 1), rows)]
    turn = jax.random.randint(jax.random.fold_in(own, 2), (rows, 1), 0, top)
    return jnp.take_along_axis(listing, (jnp.arange(top)[None, :] + turn) % top, axis=1)


def shares(amount, total, most, slope, full):
    weights = [(1 << 20) // math.isqrt(rank ** slope) + 1 for rank in range(1, amount + 1)]
    largest = most if full else min(most, max(-(-total // amount), total * weights[0] // sum(weights)))
    least = 1 if total - largest >= amount - 1 else 0
    holding, rest = [largest] + [least] * (amount - 1), total - largest - least * (amount - 1)
    while rest > 0:
        free = [i for i in range(1, amount) if holding[i] < largest] or [i for i in range(1, amount) if holding[i] < most]
        pool, budget = sum([weights[i] for i in free]), rest
        for i in free:
            extra = min(most - holding[i], max(1, budget * weights[i] // pool), rest)
            holding[i] = holding[i] + extra
            rest = rest - extra
    return np.array(holding)


def bell_draw(stream_key, shape, width, most, pieces=(), kind=jnp.bfloat16):
    gain = block_levels(stream_key, shape, pieces, -0.22, 0.18) if pieces else 1.0
    result = jax.random.normal(stream_key, shape, jnp.float32) * width * gain
    return jnp.minimum(jnp.maximum(result, -most), most).astype(kind)


def setup_inputs(seed: int = 0) -> dict:
    splits = jax.random.split(jax.random.key(seed), 12)
    prefill_q = draw_prefill_q(jax.random.fold_in(splits[11], 71), 0)
    prefill_k = draw_prefill_k(jax.random.fold_in(splits[11], 71), 0)
    prefill_v = bell_draw(splits[2], (N_GRP * CH, KVH * HD), 1.0, 6.0, ((0, 64), (1, 8)))
    span_offset = plant(jax.random.randint(splits[3], (N_GRP,), 0, 32768 - CH + 1), jax.random.fold_in(splits[3], 1), 0, 32768 - CH).astype(jnp.int32)
    page_group_keys = jax.random.split(jax.random.fold_in(splits[4], 1), (N_GRP * PCH) // PCH)
    page_group_turns = jax.random.permutation(jax.random.fold_in(splits[4], 3), (N_GRP * PCH) // PCH)
    page_group = jax.vmap(lambda own, number: deal_out(jax.random.fold_in(splits[4], 2), own, number, PCH, N_GRP, 1, CAP, 2))(page_group_keys, page_group_turns).reshape((N_GRP * PCH, 1))
    page_request = plant(jax.random.randint(splits[5], (N_GRP * PCH,), 0, REQ), jax.random.fold_in(splits[5], 1), 0, REQ - 1).astype(jnp.int32)
    decode_q = draw_decode_q(jax.random.fold_in(splits[11], 71), 0)
    cache_k = draw_cache_k(jax.random.fold_in(splits[11], 71), 0)
    cache_v = bell_draw(splits[8], (REQUESTS, LRES, KVH * HD), 1.0, 6.0, ((0, 64), (2, 8)))
    cache_len = draw_cache_len(jax.random.fold_in(splits[11], 71), 0)
    out_weight = bell_draw(splits[10], (QH * HD, D), (QH * HD) ** -0.5, 0.09375, ((0, 8), (1, 64)))
    return {"prefill_q": prefill_q, "prefill_k": prefill_k, "prefill_v": prefill_v, "span_offset": span_offset, "page_group": page_group, "page_request": page_request, "decode_q": decode_q, "cache_k": cache_k, "cache_v": cache_v, "cache_len": cache_len, "out_weight": out_weight}


rope_base = 500000.0
neg_large = -1e+30

def rotate(values, positions):
    half_dim = values.shape[-1] // 2
    frequency = rope_base ** (-2.0 * jnp.arange(half_dim, dtype=jnp.float32) / values.shape[-1])
    angle_rad = positions.astype(jnp.float32)[:, None] * frequency[None, :]
    cosine = jnp.cos(angle_rad)[:, None, :]
    sine_part = jnp.sin(angle_rad)[:, None, :]
    lower_half = values[..., :half_dim]
    upper_half = values[..., half_dim:]
    return jnp.concatenate([lower_half * cosine - upper_half * sine_part, upper_half * cosine + lower_half * sine_part], axis=-1)

def prefill_group(operands):
    query_rows, key_rows, value_rows, offset_one = operands
    positions = offset_one + jnp.arange(CH, dtype=jnp.int32)
    query_rot = rotate(query_rows.astype(jnp.float32).reshape(CH, QH, HD), positions).astype(jnp.bfloat16)
    key_rot = rotate(key_rows.astype(jnp.float32).reshape(CH, KVH, HD), positions).astype(jnp.bfloat16)
    grouped = query_rot.reshape(CH, KVH, QPK, HD).astype(jnp.float32)
    scores = jnp.einsum('qkgd,skd->kgqs', grouped, key_rot.astype(jnp.float32)) * (1.0 / math.sqrt(HD))
    query_place = jnp.arange(CH, dtype=jnp.int32)
    causal = query_place[None, :] <= query_place[:, None]
    scores = jnp.where(causal, scores, neg_large)
    peak_score = lax.optimization_barrier(jnp.max(scores, axis=-1, keepdims=True))
    weights = jnp.exp(scores - peak_score)
    weights = (weights / lax.optimization_barrier(jnp.sum(weights, axis=-1, keepdims=True))).astype(jnp.bfloat16)
    values = value_rows.reshape(CH, KVH, HD).astype(jnp.float32)
    output = jnp.einsum('kgqs,skd->qkgd', weights.astype(jnp.float32), values)
    return (output.reshape(CH, QH * HD).astype(jnp.bfloat16), key_rot.reshape(CH, KVH * HD))

def reference(prefill_q, prefill_k, prefill_v, span_offset, page_group, page_request, decode_q, cache_k, cache_v, cache_len, out_weight):
    outputs, new_keys = lax.map(prefill_group, (prefill_q.reshape(N_GRP, CH, QH * HD), prefill_k.reshape(N_GRP, CH, KVH * HD), prefill_v.reshape(N_GRP, CH, KVH * HD), span_offset))
    prefill_out = outputs.reshape(N_GRP * CH, QH * HD)
    target = page_group[:, 0].reshape(N_GRP, PCH)
    page_index = jnp.arange(PCH, dtype=jnp.int32)
    same_target = target[:, None, :] == target[:, :, None]
    earlier = lax.optimization_barrier(jnp.sum((same_target & (page_index[None, None, :] < page_index[None, :, None])).astype(jnp.int32), axis=2))
    source = jnp.broadcast_to(jnp.arange(N_GRP, dtype=jnp.int32)[:, None], (N_GRP, PCH))
    global_page = source * PCH + page_index[None, :]
    table = jnp.full((N_GRP, N_GRP, CAP), -1, jnp.int32).at[target, source, earlier].set(global_page)
    page_keys = new_keys.reshape(N_GRP * PCH, PAGE, KVH * HD)
    page_values = prefill_v.reshape(N_GRP * PCH, PAGE, KVH * HD)
    score_scale = 1.0 / math.sqrt(HD)

    def decode_group(operands):
        slots, query_rows, keys_home, values_home, lengths = operands
        live = slots >= 0
        chosen = jnp.where(live, slots, 0)
        far_keys = page_keys[chosen].reshape(N_GRP * CAP * PAGE, KVH, HD).astype(jnp.float32)
        far_values = page_values[chosen].reshape(N_GRP * CAP * PAGE, KVH, HD).astype(jnp.float32)
        owner_req = jnp.repeat(jnp.where(live, page_request[chosen], -1).reshape(-1), PAGE)
        queries = query_rows.reshape(REQ, KVH, QPK, HD).astype(jnp.float32)
        near_keys = keys_home.reshape(REQ, LRES, KVH, HD).astype(jnp.float32)
        near_values = values_home.reshape(REQ, LRES, KVH, HD).astype(jnp.float32)
        near = jnp.einsum('rkgd,rtkd->rkgt', queries, near_keys) * score_scale
        remote = jnp.einsum('rkgd,nkd->rkgn', queries, far_keys) * score_scale
        near_mask = jnp.arange(LRES, dtype=jnp.int32)[None, :] < lengths[:, None]
        remote_mask = owner_req[None, :] == jnp.arange(REQ, dtype=jnp.int32)[:, None]
        scores = jnp.concatenate([jnp.where(near_mask[:, None, None, :], near, neg_large), jnp.where(remote_mask[:, None, None, :], remote, neg_large)], axis=-1)
        peak_score = lax.optimization_barrier(jnp.max(scores, axis=-1, keepdims=True))
        weights = jnp.exp(scores - peak_score)
        weights = weights / lax.optimization_barrier(jnp.sum(weights, axis=-1, keepdims=True))
        output = jnp.einsum('rkgt,rtkd->rkgd', weights[..., :LRES], near_values) + jnp.einsum('rkgn,nkd->rkgd', weights[..., LRES:], far_values)
        return output.reshape(REQ, QH * HD).astype(jnp.bfloat16)
    attention = lax.map(decode_group, (table, decode_q.reshape(N_GRP, REQ, QH * HD), cache_k.reshape(N_GRP, REQ, LRES, KVH * HD), cache_v.reshape(N_GRP, REQ, LRES, KVH * HD), cache_len.reshape(N_GRP, REQ)))
    attention = attention.reshape(REQUESTS, QH * HD)
    decode_out = jnp.dot(attention, out_weight, preferred_element_type=jnp.float32).astype(jnp.bfloat16)
    return (prefill_out, decode_out)
```

```python
import math

import jax
import jax.numpy as jnp
from jax import lax
from jax.sharding import PartitionSpec as P

HD = 128
QPK = 4
PAGE = 16


rope_base = 500000.0
neg_large = -1e30


def rotate(values, positions):
    half_dim = values.shape[-1] // 2
    frequency = rope_base ** (-2.0 * jnp.arange(half_dim, dtype=jnp.float32) / values.shape[-1])
    angle_rad = positions.astype(jnp.float32)[:, None] * frequency[None, :]
    cosine = jnp.cos(angle_rad)[:, None, :]
    sine_part = jnp.sin(angle_rad)[:, None, :]
    lower_half = values[..., :half_dim]
    upper_half = values[..., half_dim:]
    return jnp.concatenate(
        [
            lower_half * cosine - upper_half * sine_part,
            upper_half * cosine + lower_half * sine_part,
        ],
        axis=-1,
    )


def partial_softmax(queries, keys, values, visible):
    score_scale = 1.0 / math.sqrt(HD)
    scores = (
        jnp.einsum("brkgd,bskd->brkgs", queries, keys, preferred_element_type=jnp.float32)
        * score_scale
    )
    key_shown = visible[:, :, None, None, :]
    peak_score = jnp.max(jnp.where(key_shown, scores, neg_large), axis=-1)
    weights = jnp.where(key_shown, jnp.exp(scores - peak_score[..., None]), 0.0)
    total_weight = jnp.sum(weights, axis=-1)
    summed = jnp.einsum("brkgs,bskd->brkgd", weights, values.astype(jnp.float32))
    return (peak_score, total_weight, summed)


def combine(peaks, totals, sums):
    top_peak = jnp.max(peaks, axis=0)
    factor = jnp.exp(peaks - top_peak[None])
    return jnp.sum(factor[..., None] * sums, axis=0) / jnp.sum(factor * totals, axis=0)[..., None]


def on_device(
    prefill_q,
    prefill_k,
    prefill_v,
    span_offset,
    page_group,
    page_request,
    decode_q,
    cache_k,
    cache_v,
    cache_len,
    out_weight,
):
    row_count = prefill_q.shape[0]
    key_heads = prefill_k.shape[1] // HD
    positions = span_offset[0] + jnp.arange(row_count, dtype=jnp.int32)
    query_rot = rotate(
        prefill_q.astype(jnp.float32).reshape(row_count, key_heads * QPK, HD), positions
    ).astype(jnp.bfloat16)
    key_rot = rotate(
        prefill_k.astype(jnp.float32).reshape(row_count, key_heads, HD), positions
    ).astype(jnp.bfloat16)
    value_rows = prefill_v.reshape(row_count, key_heads, HD)
    block_rows = min(row_count, 512)
    block_count = row_count // block_rows
    query_blocks = query_rot.reshape(block_count, block_rows, key_heads, QPK, HD)
    key_place = jnp.arange(row_count, dtype=jnp.int32)

    def attend(block_item):
        query_block, first_row = block_item
        scores = jnp.einsum(
            "qkgd,skd->kgqs", query_block, key_rot, preferred_element_type=jnp.float32
        ) * (1.0 / math.sqrt(HD))
        query_place = first_row + jnp.arange(block_rows, dtype=jnp.int32)
        causal = key_place[None, :] <= query_place[:, None]
        scores = jnp.where(causal, scores, neg_large)
        peak_score = jnp.max(scores, axis=-1, keepdims=True)
        weights = jnp.exp(scores - peak_score)
        weights_low = (weights / jnp.sum(weights, axis=-1, keepdims=True)).astype(jnp.bfloat16)
        return jnp.einsum(
            "kgqs,skd->qkgd", weights_low, value_rows, preferred_element_type=jnp.float32
        ).astype(jnp.bfloat16)

    starts = jnp.arange(block_count, dtype=jnp.int32) * block_rows
    prefill_out = lax.map(attend, (query_blocks, starts)).reshape(row_count, key_heads * QPK * HD)
    groups = lax.axis_size("grp")
    page_count = row_count // PAGE
    capacity = max(2, 2 * page_count // groups)
    target = page_group[:, 0]
    page_index = jnp.arange(page_count, dtype=jnp.int32)
    same_target = target[None, :] == target[:, None]
    earlier = jnp.sum(
        (same_target & (page_index[None, :] < page_index[:, None])).astype(jnp.int32), axis=1
    )
    slot_index = target * capacity + earlier
    placing = jnp.arange(groups * capacity, dtype=jnp.int32)[:, None] == slot_index[None, :]
    onehot = placing.astype(jnp.bfloat16)
    page_width = PAGE * key_heads * HD
    send_k = (
        jnp.dot(onehot, key_rot.reshape(page_count, page_width), preferred_element_type=jnp.float32)
        .astype(jnp.bfloat16)
        .reshape(groups, capacity, page_width)
    )
    send_v = (
        jnp.dot(
            onehot, prefill_v.reshape(page_count, page_width), preferred_element_type=jnp.float32
        )
        .astype(jnp.bfloat16)
        .reshape(groups, capacity, page_width)
    )
    send_req = (
        jnp.sum(placing.astype(jnp.int32) * (page_request + 1)[None, :], axis=1) - 1
    ).reshape(groups, capacity)
    requests = decode_q.shape[0]
    slot_total = cache_k.shape[1]
    queries = decode_q.reshape(requests, key_heads, QPK, HD)
    keys_home = cache_k.reshape(requests, slot_total, key_heads, HD)
    values_home = cache_v.reshape(requests, slot_total, key_heads, HD)
    visible_home = (jnp.arange(slot_total, dtype=jnp.int32)[None, :] < cache_len[:, None])[
        :, None, :
    ]
    resident = partial_softmax(queries[:, None], keys_home, values_home, visible_home)
    resident = tuple((jnp.swapaxes(member, 0, 1) for member in resident))
    request_ids = jnp.arange(requests, dtype=jnp.int32)
    owner_lanes = jnp.broadcast_to(
        send_req.astype(jnp.bfloat16)[..., None], (groups, capacity, HD)
    )
    packet = jnp.concatenate([send_k, send_v, owner_lanes], axis=-1)
    got = lax.all_to_all(packet, "grp", split_axis=0, concat_axis=0, tiled=True)
    got_k = got[..., :page_width]
    got_v = got[..., page_width : 2 * page_width]
    got_req = got[..., 2 * page_width].astype(jnp.int32)
    tokens = groups * capacity * PAGE
    new_keys = got_k.reshape(1, tokens, key_heads, HD)
    new_values = got_v.reshape(1, tokens, key_heads, HD)
    owner_req = jnp.repeat(got_req.reshape(-1), PAGE)
    visible = (owner_req[None, :] == request_ids[:, None])[None]
    remote = partial_softmax(queries[None], new_keys, new_values, visible)
    attention = combine(
        jnp.concatenate([resident[0], remote[0]], axis=0),
        jnp.concatenate([resident[1], remote[1]], axis=0),
        jnp.concatenate([resident[2], remote[2]], axis=0),
    )
    attention = attention.reshape(requests, key_heads * QPK * HD).astype(jnp.bfloat16)
    width = attention.shape[1]
    repeated = jnp.broadcast_to(attention[None], (groups, requests, width))
    everyone = lax.all_to_all(repeated, "grp", split_axis=0, concat_axis=0, tiled=True)
    term_rows = jnp.dot(
        everyone.reshape(groups * requests, width),
        out_weight,
        preferred_element_type=jnp.float32,
    ).astype(jnp.bfloat16)
    shards = lax.axis_size("tp")
    terms = lax.all_to_all(
        term_rows.reshape(shards, groups * requests // shards, term_rows.shape[1]),
        "tp",
        split_axis=0,
        concat_axis=0,
        tiled=True,
    )
    decode_out = jnp.sum(terms.astype(jnp.float32), axis=0).astype(jnp.bfloat16)
    return (prefill_out, decode_out)


def solution(mesh):
    in_specs = (
        P("grp", "tp"),
        P("grp", "tp"),
        P("grp", "tp"),
        P("grp"),
        P("grp", None),
        P("grp"),
        P("grp", "tp"),
        P("grp", None, "tp"),
        P("grp", None, "tp"),
        P("grp"),
        P("tp", "grp"),
    )
    out_specs = (P("grp", "tp"), P("tp", "grp"))
    return jax.shard_map(
        on_device, mesh=mesh, in_specs=in_specs, out_specs=out_specs, check_vma=False
    )
```

```python
import math

import jax
import jax.numpy as jnp
from jax import lax
from jax.experimental import pallas as pl
from jax.experimental.pallas import tpu as pltpu
from jax.sharding import Mesh, PartitionSpec as P

HD = 128
QPK = 4
PAGE = 16
CAP = 2
REQ = 4
ROWS = QPK * REQ

rope_base = 500000.0
neg_large = -1e30
scale = 1.0 / math.sqrt(HD)
f32 = jnp.float32
bf16 = jnp.bfloat16
vmem_limit = 32 * 1024 * 1024


def rotate(values, positions):
    half_dim = values.shape[-1] // 2
    frequency = rope_base ** (-2.0 * jnp.arange(half_dim, dtype=f32) / values.shape[-1])
    angle_rad = positions.astype(f32)[:, None] * frequency[None, :]
    cosine = jnp.cos(angle_rad)[:, None, :]
    sine_part = jnp.sin(angle_rad)[:, None, :]
    lower_half = values[..., :half_dim]
    upper_half = values[..., half_dim:]
    return jnp.concatenate(
        [
            lower_half * cosine - upper_half * sine_part,
            upper_half * cosine + lower_half * sine_part,
        ],
        axis=-1,
    )


def dot(a, b, dims):
    return lax.dot_general(a, b, (dims, ((), ())), preferred_element_type=f32)


def iota(shape, axis):
    return lax.broadcasted_iota(jnp.int32, shape, axis)


def call(kernel, outs, *args):
    return pl.pallas_call(
        kernel,
        out_shape=outs,
        compiler_params=pltpu.CompilerParams(vmem_limit_bytes=vmem_limit),
    )(*args)


def resident_kernel(q_ref, k_ref, v_ref, len_ref, sum_ref, peak_ref, total_ref):
    q = q_ref[...].astype(f32)
    rows = jnp.concatenate([q[:, h * HD : (h + 1) * HD] for h in range(QPK)], axis=0).astype(bf16)
    slots = k_ref.shape[1]
    request = iota((ROWS, 1), 0) % REQ
    live = jnp.zeros((ROWS, 1), jnp.int32)
    scores = jnp.zeros((ROWS, slots), f32)
    for r in range(REQ):
        live = jnp.where(request == r, len_ref[:, r : r + 1], live)
        scores = jnp.where(request == r, dot(rows, k_ref[r], ((1,), (1,))), scores)
    shown = iota((ROWS, slots), 1) < live
    scores = jnp.where(shown, scores * scale, neg_large)
    peak = jnp.max(scores, axis=1, keepdims=True)
    weights = jnp.where(shown, jnp.exp(scores - peak), 0.0)
    total = jnp.sum(weights, axis=1, keepdims=True)
    low = weights.astype(bf16)
    summed = jnp.zeros((ROWS, HD), f32)
    for r in range(REQ):
        summed = jnp.where(request == r, dot(low, v_ref[r], ((1,), (0,))), summed)
    sum_ref[...] = summed
    peak_ref[...] = jnp.broadcast_to(peak, (ROWS, HD))
    total_ref[...] = jnp.broadcast_to(total, (ROWS, HD))


def parts_of(value, count):
    parts = []
    for _ in range(count):
        part = value.astype(bf16).astype(f32)
        parts.append(part)
        value = value - part
    return parts


def page_kernel(q_ref, k_ref, v_ref, owner_ref, slot_ref, place_ref, out_ref):
    pages = owner_ref.shape[0]
    tokens = k_ref.shape[0]
    chosen = (iota((pages, q_ref.shape[0]), 1) == owner_ref[...]).astype(f32).astype(bf16)
    queries = dot(chosen, q_ref[...], ((1,), (0,))).astype(bf16)
    own = (iota((pages, tokens), 1) // PAGE) == iota((pages, tokens), 0)
    lane = iota((pages, HD), 1)
    extra = jnp.where(lane // ROWS == 5, place_ref[...].astype(f32), 0.0)
    columns = []
    for h in range(QPK):
        scores = dot(queries[:, h * HD : (h + 1) * HD], k_ref[...], ((1,), (1,))) * scale
        scores = jnp.where(own, scores, neg_large)
        peak = jnp.max(scores, axis=1, keepdims=True)
        weights = jnp.where(own, jnp.exp(scores - peak), 0.0)
        total = jnp.sum(weights, axis=1, keepdims=True)
        columns.append(dot(weights.astype(bf16), v_ref[...], ((1,), (0,))) / total)
        for block, part in enumerate(parts_of(peak, 3) + parts_of(total, 2)):
            extra = jnp.where(lane // REQ == block * QPK + h, part, extra)
    payload = jnp.concatenate(columns + [extra], axis=1).astype(bf16)
    placing = (iota((pages, out_ref.shape[0]), 1) == slot_ref[...]).astype(f32).astype(bf16)
    out_ref[...] = dot(placing, payload, ((0,), (0,))).astype(bf16)


def combine_kernel(got_ref, sum_ref, peak_ref, total_ref, out_ref):
    slots = got_ref.shape[0]
    extra = got_ref[:, QPK * HD :].astype(f32)
    block = [extra] + [pltpu.roll(extra, HD - ROWS * i, 1) for i in range(1, 6)]
    lane = iota((slots, HD), 1)
    shown = (block[5] == (lane % REQ + 1).astype(f32)) & (lane < ROWS)
    peaks = jnp.where(shown, block[0] + block[1] + block[2], neg_large)
    totals = block[3] + block[4]
    eye = iota((ROWS, HD), 0) == iota((ROWS, HD), 1)
    home_peak = jnp.sum(jnp.where(eye, peak_ref[...], 0.0), axis=0, keepdims=True)
    home_total = jnp.sum(jnp.where(eye, total_ref[...], 0.0), axis=0, keepdims=True)
    top = jnp.maximum(jnp.max(peaks, axis=0, keepdims=True), home_peak)
    weights = jnp.where(shown, jnp.exp(peaks - top) * totals, 0.0)
    home = jnp.exp(home_peak - top)
    whole = jnp.sum(weights, axis=0, keepdims=True) + home * home_total
    whole = jnp.where(iota((1, HD), 1) < ROWS, whole, 1.0)
    low = (weights / whole).astype(bf16)[:, :ROWS]
    home_column = jnp.sum(jnp.where(eye, home / whole, 0.0), axis=1, keepdims=True)
    rows = sum_ref[...] * home_column
    head = iota((ROWS, HD), 0) // REQ
    for h in range(QPK):
        add = dot(low, got_ref[:, h * HD : (h + 1) * HD], ((0,), (0,)))
        rows = rows + jnp.where(head == h, add, 0.0)
    wide = jnp.concatenate([rows[h * REQ : (h + 1) * REQ, :] for h in range(QPK)], axis=1)
    out_ref[...] = jnp.broadcast_to(wide[None], out_ref.shape).astype(bf16)


def on_device(
    prefill_q,
    prefill_k,
    prefill_v,
    span_offset,
    page_group,
    page_request,
    decode_q,
    cache_k,
    cache_v,
    cache_len,
    out_weight,
):
    grp = ("y", "x", "c")
    groups = lax.axis_size(grp)
    row_count = prefill_q.shape[0]
    width = decode_q.shape[1]

    asked = lax.all_to_all(
        jnp.broadcast_to(decode_q[None], (groups,) + decode_q.shape),
        grp,
        split_axis=0,
        concat_axis=0,
        tiled=True,
    ).reshape(groups * REQ, width)

    steps = lax.axis_size("x")
    here = lax.axis_index("x")
    pieces = [out_weight] + [
        lax.ppermute(out_weight, "x", [((i + k) % steps, i) for i in range(steps)])
        for k in range(1, steps)
    ]
    columns = jnp.roll(jnp.stack(pieces), here, axis=0)

    positions = span_offset[0] + jnp.arange(row_count, dtype=jnp.int32)
    key_rot = rotate(prefill_k.astype(f32).reshape(row_count, 1, HD), positions).astype(bf16)
    query_rot = rotate(prefill_q.astype(f32).reshape(row_count, QPK, HD), positions).astype(bf16)
    scores = jnp.einsum("qgd,sd->gqs", query_rot, key_rot[:, 0], preferred_element_type=f32) * scale
    place = jnp.arange(row_count, dtype=jnp.int32)
    scores = jnp.where(place[None, :] <= place[:, None], scores, neg_large)
    weights = jnp.exp(scores - jnp.max(scores, axis=-1, keepdims=True))
    weights_low = (weights / jnp.sum(weights, axis=-1, keepdims=True)).astype(bf16)
    prefill_out = (
        jnp.einsum("gqs,sd->qgd", weights_low, prefill_v, preferred_element_type=f32)
        .astype(bf16)
        .reshape(row_count, QPK * HD)
    )

    target = page_group[:, 0]
    page_index = jnp.arange(target.shape[0], dtype=jnp.int32)
    same_target = target[None, :] == target[:, None]
    earlier = jnp.sum(
        (same_target & (page_index[None, :] < page_index[:, None])).astype(jnp.int32), axis=1
    )
    slot_index = (target * CAP + earlier)[:, None]
    owner = (target * REQ + page_request)[:, None]

    rows_of = jax.ShapeDtypeStruct((ROWS, HD), f32)
    home = call(
        resident_kernel, (rows_of,) * 3, decode_q, cache_k, cache_v, cache_len.reshape(1, REQ)
    )
    sent = call(
        page_kernel,
        jax.ShapeDtypeStruct((groups * CAP, width + HD), bf16),
        asked,
        key_rot[:, 0],
        prefill_v,
        owner,
        slot_index,
        (page_request + 1)[:, None],
    )
    got = lax.all_to_all(
        sent.reshape(groups, CAP, width + HD), grp, split_axis=0, concat_axis=0, tiled=True
    ).reshape(groups * CAP, width + HD)

    peers = lax.axis_size(("y", "c"))
    repeated = call(
        combine_kernel, jax.ShapeDtypeStruct((peers, REQ, width), bf16), got, *home
    )
    everyone = lax.all_to_all(repeated, ("y", "c"), split_axis=0, concat_axis=0, tiled=True)
    everyone = everyone.reshape(peers * REQ, width)
    shards = lax.axis_size("z")
    terms = jnp.einsum("ad,xdc->xac", everyone, columns, preferred_element_type=f32).astype(bf16)
    terms = terms.reshape(steps * shards, peers * REQ // shards, HD)
    terms = lax.all_to_all(terms, ("x", "z"), split_axis=0, concat_axis=0, tiled=True)
    terms = terms.reshape(steps, shards, peers * REQ // shards, HD)
    decode_out = jnp.sum(terms.astype(f32), axis=1).astype(bf16).reshape(-1, HD)
    return (prefill_out, decode_out)


def solution(mesh):
    fine = Mesh(mesh.devices.reshape(8, 4, 2, 8), ("y", "x", "c", "z"))
    grp = ("y", "x", "c")
    in_specs = (
        P(grp, "z"),
        P(grp, "z"),
        P(grp, "z"),
        P(grp),
        P(grp, None),
        P(grp),
        P(grp, "z"),
        P(grp, None, "z"),
        P(grp, None, "z"),
        P(grp),
        P("z", grp),
    )
    out_specs = (P(grp, "z"), P("z", grp))
    return jax.shard_map(
        on_device, mesh=fine, in_specs=in_specs, out_specs=out_specs, check_vma=False
    )
```

```python
import math

import jax
import jax.numpy as jnp
from jax import lax
from jax.experimental import pallas as pl
from jax.experimental.pallas import tpu as pltpu
from jax.sharding import Mesh, PartitionSpec as P

HD = 128
QPK = 4
PAGE = 16
CAP = 2
REQ = 4
ROWS = QPK * REQ

rope_base = 500000.0
neg_large = -1e30
scale = 1.0 / math.sqrt(HD)
f32 = jnp.float32
bf16 = jnp.bfloat16
vmem_limit = 32 * 1024 * 1024


def angles(offset, row_count):
    lane = jnp.arange(HD, dtype=jnp.int32)
    frequency = rope_base ** (-2.0 * (lane % (HD // 2)).astype(f32) / HD)
    positions = offset + jnp.arange(row_count, dtype=jnp.int32)
    angle_rad = positions.astype(f32)[:, None] * frequency[None, :]
    sign = jnp.where(lane < HD // 2, -1.0, 1.0)
    return jnp.cos(angle_rad), jnp.sin(angle_rad) * sign[None, :]


def dot(a, b, dims):
    return lax.dot_general(a, b, (dims, ((), ())), preferred_element_type=f32)


def iota(shape, axis):
    return lax.broadcasted_iota(jnp.int32, shape, axis)


def call(kernel, outs, *args):
    return pl.pallas_call(
        kernel,
        out_shape=outs,
        compiler_params=pltpu.CompilerParams(vmem_limit_bytes=vmem_limit),
    )(*args)


def prefill_kernel(q_ref, k_ref, v_ref, cos_ref, sin_ref, out_ref, key_ref):
    rows = k_ref.shape[0]
    cosine, sine_part = cos_ref[...], sin_ref[...]

    def rotate(values):
        values = values.astype(f32)
        turned = pltpu.roll(values, HD // 2, 1)
        return (values * cosine + turned * sine_part).astype(bf16)

    keys = rotate(k_ref[...])
    key_ref[...] = keys
    causal = iota((rows, rows), 1) <= iota((rows, rows), 0)
    for h in range(QPK):
        part = slice(h * HD, (h + 1) * HD)
        scores = dot(rotate(q_ref[:, part]), keys, ((1,), (1,))) * scale
        scores = jnp.where(causal, scores, neg_large)
        weights = jnp.exp(scores - jnp.max(scores, axis=1, keepdims=True))
        weights = weights * (1.0 / jnp.sum(weights, axis=1, keepdims=True))
        out_ref[:, part] = dot(weights.astype(bf16), v_ref[...], ((1,), (0,))).astype(bf16)


def resident_kernel(q_ref, k_ref, v_ref, len_ref, sum_ref, peak_ref, total_ref):
    q = q_ref[...].astype(f32)
    rows = jnp.concatenate([q[:, h * HD : (h + 1) * HD] for h in range(QPK)], axis=0).astype(bf16)
    slots = k_ref.shape[1]
    request = iota((ROWS, 1), 0) % REQ
    live = jnp.zeros((ROWS, 1), jnp.int32)
    scores = jnp.zeros((ROWS, slots), f32)
    for r in range(REQ):
        live = jnp.where(request == r, len_ref[:, r : r + 1], live)
        scores = jnp.where(request == r, dot(rows, k_ref[r], ((1,), (1,))), scores)
    shown = iota((ROWS, slots), 1) < live
    scores = jnp.where(shown, scores * scale, neg_large)
    peak = jnp.max(scores, axis=1, keepdims=True)
    weights = jnp.where(shown, jnp.exp(scores - peak), 0.0)
    total = jnp.sum(weights, axis=1, keepdims=True)
    low = weights.astype(bf16)
    summed = jnp.zeros((ROWS, HD), f32)
    for r in range(REQ):
        summed = jnp.where(request == r, dot(low, v_ref[r], ((1,), (0,))), summed)
    sum_ref[...] = summed
    peak_ref[...] = jnp.broadcast_to(peak, (ROWS, HD))
    total_ref[...] = jnp.broadcast_to(total, (ROWS, HD))


def repeat_kernel(q_ref, out_ref):
    out_ref[...] = jnp.broadcast_to(q_ref[...][None], out_ref.shape)


def parts_of(value, count):
    parts = []
    for _ in range(count):
        part = value.astype(bf16).astype(f32)
        parts.append(part)
        value = value - part
    return parts


def page_kernel(q_ref, k_ref, v_ref, owner_ref, slot_ref, place_ref, out_ref):
    pages = owner_ref.shape[0]
    tokens = k_ref.shape[0]
    chosen = (iota((pages, q_ref.shape[0]), 1) == owner_ref[...]).astype(f32).astype(bf16)
    queries = dot(chosen, q_ref[...], ((1,), (0,))).astype(bf16)
    own = (iota((pages, tokens), 1) // PAGE) == iota((pages, tokens), 0)
    lane = iota((pages, HD), 1)
    extra = jnp.where(lane // ROWS == 5, place_ref[...].astype(f32), 0.0)
    columns = []
    for h in range(QPK):
        scores = dot(queries[:, h * HD : (h + 1) * HD], k_ref[...], ((1,), (1,))) * scale
        scores = jnp.where(own, scores, neg_large)
        peak = jnp.max(scores, axis=1, keepdims=True)
        weights = jnp.where(own, jnp.exp(scores - peak), 0.0)
        total = jnp.sum(weights, axis=1, keepdims=True)
        columns.append(dot(weights.astype(bf16), v_ref[...], ((1,), (0,))) / total)
        for block, part in enumerate(parts_of(peak, 3) + parts_of(total, 2)):
            extra = jnp.where(lane // REQ == block * QPK + h, part, extra)
    payload = jnp.concatenate(columns + [extra], axis=1).astype(bf16)
    placing = (iota((pages, out_ref.shape[0] * CAP), 1) == slot_ref[...]).astype(f32).astype(bf16)
    placed = dot(placing, payload, ((0,), (0,)))
    out_ref[...] = placed.reshape(out_ref.shape).astype(bf16)


def combine_kernel(got_ref, sum_ref, peak_ref, total_ref, out_ref):
    slots = got_ref.shape[0]
    extra = got_ref[:, QPK * HD :].astype(f32)
    block = [extra] + [pltpu.roll(extra, HD - ROWS * i, 1) for i in range(1, 6)]
    lane = iota((slots, HD), 1)
    shown = (block[5] == (lane % REQ + 1).astype(f32)) & (lane < ROWS)
    peaks = jnp.where(shown, block[0] + block[1] + block[2], neg_large)
    totals = block[3] + block[4]
    eye = iota((ROWS, HD), 0) == iota((ROWS, HD), 1)
    home_peak = jnp.sum(jnp.where(eye, peak_ref[...], 0.0), axis=0, keepdims=True)
    home_total = jnp.sum(jnp.where(eye, total_ref[...], 0.0), axis=0, keepdims=True)
    top = jnp.maximum(jnp.max(peaks, axis=0, keepdims=True), home_peak)
    weights = jnp.where(shown, jnp.exp(peaks - top) * totals, 0.0)
    home = jnp.exp(home_peak - top)
    whole = jnp.sum(weights, axis=0, keepdims=True) + home * home_total
    whole = jnp.where(iota((1, HD), 1) < ROWS, whole, 1.0)
    low = (weights / whole).astype(bf16)[:, :ROWS]
    home_column = jnp.sum(jnp.where(eye, home / whole, 0.0), axis=1, keepdims=True)
    rows = sum_ref[...] * home_column
    head = iota((ROWS, HD), 0) // REQ
    for h in range(QPK):
        add = dot(low, got_ref[:, h * HD : (h + 1) * HD], ((0,), (0,)))
        rows = rows + jnp.where(head == h, add, 0.0)
    wide = jnp.concatenate([rows[h * REQ : (h + 1) * REQ, :] for h in range(QPK)], axis=1)
    out_ref[...] = jnp.broadcast_to(wide[None], out_ref.shape).astype(bf16)


def sum_kernel(terms_ref, out_ref):
    half = terms_ref.shape[0] // 2
    sums = []
    for c in range(2):
        total = terms_ref[c * half].astype(f32)
        for t in range(1, half):
            total = total + terms_ref[c * half + t].astype(f32)
        sums.append(total)
    blocks = []
    for x in range(terms_ref.shape[1] // REQ):
        blocks += [sums[c][x * REQ : (x + 1) * REQ] for c in range(2)]
    out_ref[...] = jnp.concatenate(blocks, axis=0).astype(bf16)


def on_device(
    prefill_q,
    prefill_k,
    prefill_v,
    span_offset,
    page_group,
    page_request,
    decode_q,
    cache_k,
    cache_v,
    cache_len,
    out_weight,
):
    grp = ("y", "x", "c")
    groups = lax.axis_size(grp)
    row_count = prefill_q.shape[0]
    width = decode_q.shape[1]

    asked = lax.all_to_all(
        call(repeat_kernel, jax.ShapeDtypeStruct((groups,) + decode_q.shape, bf16), decode_q),
        grp,
        split_axis=0,
        concat_axis=0,
        tiled=True,
    ).reshape(groups * REQ, width)

    cosine, sine_part = angles(span_offset[0], row_count)
    prefill_out, key_rot = call(
        prefill_kernel,
        (
            jax.ShapeDtypeStruct(prefill_q.shape, bf16),
            jax.ShapeDtypeStruct(prefill_k.shape, bf16),
        ),
        prefill_q,
        prefill_k,
        prefill_v,
        cosine,
        sine_part,
    )
    key_rot, own_weight = lax.optimization_barrier((key_rot, out_weight))
    other_weight = lax.ppermute(own_weight, "c", [(0, 1), (1, 0)])
    first = lax.axis_index("c") == 0
    columns = jnp.stack(
        [
            jnp.where(first, own_weight, other_weight),
            jnp.where(first, other_weight, own_weight),
        ]
    )

    target = page_group[:, 0]
    page_index = jnp.arange(target.shape[0], dtype=jnp.int32)
    same_target = target[None, :] == target[:, None]
    earlier = jnp.sum(
        (same_target & (page_index[None, :] < page_index[:, None])).astype(jnp.int32), axis=1
    )
    slot_index = (target * CAP + earlier)[:, None]
    owner = (target * REQ + page_request)[:, None]

    rows_of = jax.ShapeDtypeStruct((ROWS, HD), f32)
    home = call(
        resident_kernel, (rows_of,) * 3, decode_q, cache_k, cache_v, cache_len.reshape(1, REQ)
    )
    asked, prefill_out, columns, home = lax.optimization_barrier(
        (asked, prefill_out, columns, home)
    )
    sent = call(
        page_kernel,
        jax.ShapeDtypeStruct((groups, CAP, width + HD), bf16),
        asked,
        key_rot,
        prefill_v,
        owner,
        slot_index,
        (page_request + 1)[:, None],
    )
    got = lax.all_to_all(sent, grp, split_axis=0, concat_axis=0, tiled=True)
    got = got.reshape(groups * CAP, width + HD)

    peers = lax.axis_size(("y", "x"))
    repeated = call(
        combine_kernel, jax.ShapeDtypeStruct((peers, REQ, width), bf16), got, *home
    )
    everyone = lax.all_to_all(repeated, ("y", "x"), split_axis=0, concat_axis=0, tiled=True)
    everyone = everyone.reshape(peers * REQ, width)
    shards = lax.axis_size("z")
    cores = lax.axis_size("c")
    terms = jnp.einsum("ad,cde->cae", everyone, columns, preferred_element_type=f32).astype(bf16)
    terms = terms.reshape(cores * shards, peers * REQ // shards, HD)
    terms = lax.all_to_all(terms, ("c", "z"), split_axis=0, concat_axis=0, tiled=True)
    decode_out = call(
        sum_kernel, jax.ShapeDtypeStruct((peers * REQ * cores // shards, HD), bf16), terms
    )
    return (prefill_out, decode_out)


def solution(mesh):
    fine = Mesh(mesh.devices.reshape(8, 4, 2, 8), ("y", "x", "c", "z"))
    grp = ("y", "x", "c")
    in_specs = (
        P(grp, "z"),
        P(grp, "z"),
        P(grp, "z"),
        P(grp),
        P(grp, None),
        P(grp),
        P(grp, "z"),
        P(grp, None, "z"),
        P(grp, None, "z"),
        P(grp),
        P("z", grp),
    )
    out_specs = (P(grp, "z"), P("z", grp))
    return jax.shard_map(
        on_device, mesh=fine, in_specs=in_specs, out_specs=out_specs, check_vma=False
    )
```

```python
import math

import jax
import jax.numpy as jnp
from jax import lax
from jax.experimental import pallas as pl
from jax.experimental.pallas import tpu as pltpu
from jax.sharding import Mesh, PartitionSpec as P

HD = 128
QPK = 4
PAGE = 16
CAP = 2
REQ = 4
ROWS = QPK * REQ

rope_base = 500000.0
neg_large = -1e30
scale = 1.0 / math.sqrt(HD)
f32 = jnp.float32
bf16 = jnp.bfloat16
vmem_limit = 32 * 1024 * 1024
shadow_flops = 5 * 10**9
CH = 256
at_values, at_info, at_weight, at_end = CH, 2 * CH, 2 * CH + 16, 2 * CH + 16 + 512


def angles(offset, row_count):
    lane = jnp.arange(HD, dtype=jnp.int32)
    frequency = rope_base ** (-2.0 * (lane % (HD // 2)).astype(f32) / HD)
    positions = offset + jnp.arange(row_count, dtype=jnp.int32)
    angle_rad = positions.astype(f32)[:, None] * frequency[None, :]
    sign = jnp.where(lane < HD // 2, -1.0, 1.0)
    return jnp.cos(angle_rad), jnp.sin(angle_rad) * sign[None, :]


def dot(a, b, dims):
    return lax.dot_general(a, b, (dims, ((), ())), preferred_element_type=f32)


def iota(shape, axis):
    return lax.broadcasted_iota(jnp.int32, shape, axis)


def call(kernel, outs, *args, scalars=0, unread=0, flops=0):
    moved = sum(a.size * a.dtype.itemsize for a in (*args, *jax.tree.leaves(outs)))
    places = [pltpu.SMEM] * scalars + [pltpu.VMEM] * (len(args) - scalars - unread)
    places += [pl.ANY] * unread
    return pl.pallas_call(
        kernel,
        out_shape=outs,
        in_specs=[pl.BlockSpec(memory_space=place) for place in places],
        cost_estimate=pl.CostEstimate(flops=flops, bytes_accessed=moved, transcendentals=0),
        compiler_params=pltpu.CompilerParams(vmem_limit_bytes=vmem_limit),
    )(*args)


def rotate(values, cosine, sine_part):
    values = values.astype(f32)
    return (values * cosine + pltpu.roll(values, HD // 2, 1) * sine_part).astype(bf16)


def pack_kernel(
    k_ref, v_ref, cos_ref, sin_ref, group_ref, request_ref, weight_ref, _, pack_ref
):
    pack_ref[:at_values, :] = rotate(k_ref[...], cos_ref[...], sin_ref[...])
    pack_ref[at_values:at_info, :] = v_ref[...]
    pack_ref[at_weight:, :] = weight_ref[...]

    pages = group_ref.shape[1]
    eye = iota((pages, pages), 0) == iota((pages, pages), 1)
    group_row = group_ref[...].astype(f32)
    group = jnp.sum(jnp.where(eye, group_row, 0.0), axis=1, keepdims=True)
    request = jnp.sum(jnp.where(eye, request_ref[...].astype(f32), 0.0), axis=1, keepdims=True)
    before = iota((pages, pages), 1) < iota((pages, pages), 0)
    earlier = jnp.where(before & (group == group_row), 1.0, 0.0)
    earlier = jnp.sum(earlier, axis=1, keepdims=True)
    lane = iota((pages, HD), 1)
    info = jnp.where(lane == 0, group, jnp.where(lane == 1, request, earlier))
    pack_ref[at_info:at_weight, :] = info.astype(bf16)


def prefill_kernel(q_ref, pack_ref, cos_ref, sin_ref, _, out_ref):
    cosine, sine_part = cos_ref[...], sin_ref[...]
    keys, values = pack_ref[:at_values, :], pack_ref[at_values:at_info, :]
    causal = iota((CH, CH), 1) <= iota((CH, CH), 0)
    for h in range(QPK):
        part = slice(h * HD, (h + 1) * HD)
        queries = rotate(q_ref[:, part], cosine, sine_part)
        scores = dot(queries, keys, ((1,), (1,))) * scale
        scores = jnp.where(causal, scores, neg_large)
        weights = jnp.exp(scores - jnp.max(scores, axis=1, keepdims=True))
        weights = weights * (1.0 / jnp.sum(weights, axis=1, keepdims=True))
        out_ref[:, part] = dot(weights.astype(bf16), values, ((1,), (0,))).astype(bf16)


def resident_kernel(q_ref, k_ref, v_ref, len_ref, sum_ref, peak_ref, total_ref):
    q = q_ref[...].astype(f32)
    rows = jnp.concatenate([q[:, h * HD : (h + 1) * HD] for h in range(QPK)], axis=0).astype(bf16)
    slots = k_ref.shape[1]
    request = iota((ROWS, 1), 0) % REQ
    live = jnp.zeros((ROWS, 1), jnp.int32)
    scores = jnp.zeros((ROWS, slots), f32)
    for r in range(REQ):
        live = jnp.where(request == r, len_ref[:, r : r + 1], live)
        scores = jnp.where(request == r, dot(rows, k_ref[r], ((1,), (1,))), scores)
    shown = iota((ROWS, slots), 1) < live
    scores = jnp.where(shown, scores * scale, neg_large)
    peak = jnp.max(scores, axis=1, keepdims=True)
    weights = jnp.where(shown, jnp.exp(scores - peak), 0.0)
    total = jnp.sum(weights, axis=1, keepdims=True)
    low = weights.astype(bf16)
    summed = jnp.zeros((ROWS, HD), f32)
    for r in range(REQ):
        summed = jnp.where(request == r, dot(low, v_ref[r], ((1,), (0,))), summed)
    sum_ref[...] = summed
    peak_ref[...] = jnp.broadcast_to(peak, (ROWS, HD))
    total_ref[...] = jnp.broadcast_to(total, (ROWS, HD))


def repeat_kernel(q_ref, out_ref):
    out_ref[...] = jnp.broadcast_to(q_ref[...][None], out_ref.shape)


def parts_of(value, count):
    parts = []
    for _ in range(count):
        part = value.astype(bf16).astype(f32)
        parts.append(part)
        value = value - part
    return parts


def page_kernel(core_ref, q_ref, own_ref, other_ref, out_ref):
    core = core_ref[0].astype(f32)
    pages = at_weight - at_info
    slots = out_ref.shape[0] * out_ref.shape[1]
    placed = jnp.zeros((slots, out_ref.shape[2]), f32)
    own = iota((QPK * pages, CH), 1) // PAGE == iota((QPK * pages, CH), 0) % pages
    lane = iota((pages, HD), 1)
    row_lane = iota((pages, q_ref.shape[0]), 1).astype(f32)
    slot_lane = iota((pages, slots), 1).astype(f32)
    for side, ref in enumerate((own_ref, other_ref)):
        info = ref[at_info:at_weight, :].astype(f32)
        group, request, earlier = info[:, 0:1], info[:, 1:2], info[:, 2:3]
        chip = jnp.floor(group * 0.5)
        mine = group - 2.0 * chip == core
        row = jnp.where(mine, chip * REQ + request, -1.0)
        slot = jnp.where(mine, chip * (2 * CAP) + side * CAP + earlier, -1.0)
        chosen = (row_lane == row).astype(f32).astype(bf16)
        placing = (slot_lane == slot).astype(f32).astype(bf16)
        asked = dot(chosen, q_ref[...], ((1,), (0,)))
        asked = [asked[:, h * HD : (h + 1) * HD] for h in range(QPK)]
        queries = jnp.concatenate(asked, axis=0).astype(bf16)
        scores = dot(queries, ref[:at_values, :], ((1,), (1,))) * scale
        scores = jnp.where(own, scores, neg_large)
        peak = jnp.max(scores, axis=1, keepdims=True)
        weights = jnp.where(own, jnp.exp(scores - peak), 0.0)
        total = jnp.sum(weights, axis=1, keepdims=True)
        values = dot(weights.astype(bf16), ref[at_values:at_info, :], ((1,), (0,))) / total
        extra = jnp.where(lane // ROWS == 5, request + 1.0, 0.0)
        parts = parts_of(peak, 3) + parts_of(total, 2)
        columns = []
        for h in range(QPK):
            part = slice(h * pages, (h + 1) * pages)
            columns.append(values[part])
            for block, column in enumerate(parts):
                extra = jnp.where(lane // REQ == block * QPK + h, column[part], extra)
        payload = jnp.concatenate(columns + [extra], axis=1).astype(bf16)
        placed = placed + dot(placing, payload, ((0,), (0,)))
    out_ref[...] = placed.reshape(out_ref.shape).astype(bf16)


def project_kernel(core_ref, rows_ref, own_ref, other_ref, out_ref):
    core = core_ref[0]
    for index, ref in ((core, own_ref), (1 - core, other_ref)):
        product = dot(rows_ref[...], ref[at_weight:, :], ((1,), (0,)))
        out_ref[index] = product.astype(bf16)


def combine_kernel(got_ref, sum_ref, peak_ref, total_ref, out_ref):
    slots = got_ref.shape[0]
    extra = got_ref[:, QPK * HD :].astype(f32)
    block = [extra] + [pltpu.roll(extra, HD - ROWS * i, 1) for i in range(1, 6)]
    lane = iota((slots, HD), 1)
    shown = (block[5] == (lane % REQ + 1).astype(f32)) & (lane < ROWS)
    peaks = jnp.where(shown, block[0] + block[1] + block[2], neg_large)
    totals = block[3] + block[4]
    eye = iota((ROWS, HD), 0) == iota((ROWS, HD), 1)
    home_peak = jnp.sum(jnp.where(eye, peak_ref[...], 0.0), axis=0, keepdims=True)
    home_total = jnp.sum(jnp.where(eye, total_ref[...], 0.0), axis=0, keepdims=True)
    top = jnp.maximum(jnp.max(peaks, axis=0, keepdims=True), home_peak)
    weights = jnp.where(shown, jnp.exp(peaks - top) * totals, 0.0)
    home = jnp.exp(home_peak - top)
    whole = jnp.sum(weights, axis=0, keepdims=True) + home * home_total
    whole = jnp.where(iota((1, HD), 1) < ROWS, whole, 1.0)
    low = (weights / whole).astype(bf16)[:, :ROWS]
    home_column = jnp.sum(jnp.where(eye, home / whole, 0.0), axis=1, keepdims=True)
    rows = sum_ref[...] * home_column
    head = iota((ROWS, HD), 0) // REQ
    for h in range(QPK):
        add = dot(low, got_ref[:, h * HD : (h + 1) * HD], ((0,), (0,)))
        rows = rows + jnp.where(head == h, add, 0.0)
    wide = jnp.concatenate([rows[h * REQ : (h + 1) * REQ, :] for h in range(QPK)], axis=1)
    out_ref[...] = jnp.broadcast_to(wide[None], out_ref.shape).astype(bf16)


def sum_kernel(terms_ref, out_ref):
    half = terms_ref.shape[0] // 2
    sums = []
    for c in range(2):
        total = terms_ref[c * half].astype(f32)
        for t in range(1, half):
            total = total + terms_ref[c * half + t].astype(f32)
        sums.append(total)
    blocks = []
    for x in range(terms_ref.shape[1] // REQ):
        blocks += [sums[c][x * REQ : (x + 1) * REQ] for c in range(2)]
    out_ref[...] = jnp.concatenate(blocks, axis=0).astype(bf16)


def on_device(
    prefill_q,
    prefill_k,
    prefill_v,
    span_offset,
    page_group,
    page_request,
    decode_q,
    cache_k,
    cache_v,
    cache_len,
    out_weight,
):
    chips = ("y", "x")
    peers = lax.axis_size(chips)
    width = decode_q.shape[1]

    asking = call(repeat_kernel, jax.ShapeDtypeStruct((peers,) + decode_q.shape, bf16), decode_q)
    asked = lax.all_to_all(asking, chips, split_axis=0, concat_axis=0, tiled=True)
    asked = asked.reshape(peers * REQ, width)

    core = lax.axis_index("c").reshape(1)
    cosine, sine_part = angles(span_offset[0], prefill_q.shape[0])
    own = call(
        pack_kernel,
        jax.ShapeDtypeStruct((at_end, HD), bf16),
        prefill_k,
        prefill_v,
        cosine,
        sine_part,
        page_group.reshape(1, -1),
        page_request.reshape(1, -1),
        out_weight,
        asking,
        unread=1,
    )
    other = lax.ppermute(own, "c", [(0, 1), (1, 0)])

    rows_of = jax.ShapeDtypeStruct((ROWS, HD), f32)
    home = call(
        resident_kernel, (rows_of,) * 3, decode_q, cache_k, cache_v, cache_len.reshape(1, REQ), flops=shadow_flops
    )
    asked, other, home = lax.optimization_barrier((asked, other, home))
    sent = call(
        page_kernel,
        jax.ShapeDtypeStruct((peers, 2 * CAP, width + HD), bf16),
        core,
        asked,
        own,
        other,
        scalars=1,
    )
    got = lax.all_to_all(sent, chips, split_axis=0, concat_axis=0, tiled=True)
    got = got.reshape(peers * 2 * CAP, width + HD)

    repeated = call(
        combine_kernel, jax.ShapeDtypeStruct((peers, REQ, width), bf16), got, *home
    )
    everyone = lax.all_to_all(repeated, chips, split_axis=0, concat_axis=0, tiled=True)
    everyone = everyone.reshape(peers * REQ, width)
    shards = lax.axis_size("z")
    cores = lax.axis_size("c")
    terms = call(
        project_kernel,
        jax.ShapeDtypeStruct((cores, peers * REQ, HD), bf16),
        core,
        everyone,
        own,
        other,
        scalars=1,
    )
    terms = terms.reshape(cores * shards, peers * REQ // shards, HD)
    prefill_out = call(
        prefill_kernel,
        jax.ShapeDtypeStruct(prefill_q.shape, bf16),
        prefill_q,
        own,
        cosine,
        sine_part,
        terms,
        unread=1,
        flops=shadow_flops,
    )
    terms = lax.all_to_all(terms, ("c", "z"), split_axis=0, concat_axis=0, tiled=True)
    decode_out = call(
        sum_kernel, jax.ShapeDtypeStruct((peers * REQ * cores // shards, HD), bf16), terms
    )
    return (prefill_out, decode_out)


def solution(mesh):
    fine = Mesh(mesh.devices.reshape(8, 4, 2, 8), ("y", "x", "c", "z"))
    grp = ("y", "x", "c")
    in_specs = (
        P(grp, "z"),
        P(grp, "z"),
        P(grp, "z"),
        P(grp),
        P(grp, None),
        P(grp),
        P(grp, "z"),
        P(grp, None, "z"),
        P(grp, None, "z"),
        P(grp),
        P("z", grp),
    )
    out_specs = (P(grp, "z"), P("z", grp))
    return jax.shard_map(
        on_device, mesh=fine, in_specs=in_specs, out_specs=out_specs, check_vma=False
    )
```

```python
import math

import jax
import jax.numpy as jnp
from jax import lax
from jax.experimental import pallas as pl
from jax.experimental.pallas import tpu as pltpu
from jax.sharding import Mesh, PartitionSpec as P

HD = 128
QPK = 4
PAGE = 16
CAP = 2
REQ = 4
ROWS = QPK * REQ

rope_base = 500000.0
neg_large = -1e30
scale = 1.0 / math.sqrt(HD)
f32 = jnp.float32
bf16 = jnp.bfloat16
vmem_limit = 32 * 1024 * 1024
shadow_flops = 5 * 10**9
CH = 256
at_requests, at_lengths, at_offset, at_core = 16, 32, 32 + REQ, 33 + REQ
at_values, at_info, at_weight, at_end = CH, 2 * CH, 2 * CH + 16, 2 * CH + 16 + 512


def factors(offset):
    shape = (16, HD)
    lane, row = iota(shape, 1), iota(shape, 0)
    power = (lane % (HD // 2)).astype(f32) * (-2.0 / HD * math.log(rope_base))
    frequency = jnp.exp(power)
    sign = jnp.where(lane < HD // 2, -1.0, 1.0)

    def turn(position):
        angle_rad = position.astype(f32) * frequency
        return jnp.cos(angle_rad), jnp.sin(angle_rad) * sign

    fine, coarse = turn(row), turn(offset + 16 * row)
    cosine, sine_part = [], []
    for d in range(CH // 16):
        c, s = coarse[0][d : d + 1], coarse[1][d : d + 1]
        cosine.append(fine[0] * c - fine[1] * s)
        sine_part.append(fine[1] * c + fine[0] * s)
    return jnp.concatenate(cosine, axis=0), jnp.concatenate(sine_part, axis=0)


def dot(a, b, dims):
    return lax.dot_general(a, b, (dims, ((), ())), preferred_element_type=f32)


def iota(shape, axis):
    return lax.broadcasted_iota(jnp.int32, shape, axis)


def call(kernel, outs, *args, unread=0, flops=0):
    moved = sum(a.size * a.dtype.itemsize for a in (*args, *jax.tree.leaves(outs)))
    places = [pltpu.VMEM] * (len(args) - unread) + [pl.ANY] * unread
    return pl.pallas_call(
        kernel,
        out_shape=outs,
        in_specs=[pl.BlockSpec(memory_space=place) for place in places],
        cost_estimate=pl.CostEstimate(flops=flops, bytes_accessed=moved, transcendentals=0),
        compiler_params=pltpu.CompilerParams(vmem_limit_bytes=vmem_limit),
    )(*args)


def rotate(values, cosine, sine_part):
    values = values.astype(f32)
    return (values * cosine + pltpu.roll(values, HD // 2, 1) * sine_part).astype(bf16)


def pack_kernel(
    ints_ref, k_ref, v_ref, weight_ref, _, pack_ref
):
    pack_ref[:at_values, :] = rotate(k_ref[...], *factors(ints_ref[:, at_offset : at_offset + 1]))
    pack_ref[at_values:at_info, :] = v_ref[...]
    pack_ref[at_weight:, :] = weight_ref[...]

    pages = at_requests
    eye = iota((pages, pages), 0) == iota((pages, pages), 1)
    group_row = ints_ref[:, :pages].astype(f32)
    group = jnp.sum(jnp.where(eye, group_row, 0.0), axis=1, keepdims=True)
    request = jnp.sum(jnp.where(eye, ints_ref[:, at_requests:at_lengths].astype(f32), 0.0), axis=1, keepdims=True)
    before = iota((pages, pages), 1) < iota((pages, pages), 0)
    earlier = jnp.where(before & (group == group_row), 1.0, 0.0)
    earlier = jnp.sum(earlier, axis=1, keepdims=True)
    lane = iota((pages, HD), 1)
    core = ints_ref[:, at_core : at_core + 1].astype(f32)
    info = jnp.where(lane == 0, group, jnp.where(lane == 1, request, earlier))
    info = jnp.where(lane == 3, core, info)
    pack_ref[at_info:at_weight, :] = info.astype(bf16)


def prefill_kernel(ints_ref, q_ref, pack_ref, _, out_ref):
    cosine, sine_part = factors(ints_ref[:, at_offset : at_offset + 1])
    keys, values = pack_ref[:at_values, :], pack_ref[at_values:at_info, :]
    causal = iota((CH, CH), 1) <= iota((CH, CH), 0)
    for h in range(QPK):
        part = slice(h * HD, (h + 1) * HD)
        queries = rotate(q_ref[:, part], cosine, sine_part)
        scores = dot(queries, keys, ((1,), (1,))) * scale
        scores = jnp.where(causal, scores, neg_large)
        weights = jnp.exp(scores - jnp.max(scores, axis=1, keepdims=True))
        weights = weights * (1.0 / jnp.sum(weights, axis=1, keepdims=True))
        out_ref[:, part] = dot(weights.astype(bf16), values, ((1,), (0,))).astype(bf16)


def resident_kernel(rows_ref, k_ref, v_ref, ints_ref, sum_ref, peak_ref, total_ref):
    rows = rows_ref[...]
    slots = k_ref.shape[1]
    request = iota((ROWS, 1), 0) % REQ
    live = jnp.zeros((ROWS, 1), jnp.int32)
    scores = jnp.zeros((ROWS, slots), f32)
    for r in range(REQ):
        live = jnp.where(request == r, ints_ref[:, at_lengths + r : at_lengths + r + 1], live)
        scores = jnp.where(request == r, dot(rows, k_ref[r], ((1,), (1,))), scores)
    shown = iota((ROWS, slots), 1) < live
    scores = jnp.where(shown, scores * scale, neg_large)
    peak = jnp.max(scores, axis=1, keepdims=True)
    weights = jnp.where(shown, jnp.exp(scores - peak), 0.0)
    total = jnp.sum(weights, axis=1, keepdims=True)
    low = weights.astype(bf16)
    summed = jnp.zeros((ROWS, HD), f32)
    for r in range(REQ):
        summed = jnp.where(request == r, dot(low, v_ref[r], ((1,), (0,))), summed)
    sum_ref[...] = summed
    peak_ref[...] = jnp.broadcast_to(peak, (ROWS, HD))
    total_ref[...] = jnp.broadcast_to(total, (ROWS, HD))


def repeat_kernel(q_ref, out_ref, rows_ref):
    out_ref[...] = jnp.broadcast_to(q_ref[...][None], out_ref.shape)
    q = q_ref[...].astype(f32)
    rows = jnp.concatenate([q[:, h * HD : (h + 1) * HD] for h in range(QPK)], axis=0)
    rows_ref[...] = rows.astype(bf16)


def parts_of(value, count):
    parts = []
    for _ in range(count):
        part = value.astype(bf16).astype(f32)
        parts.append(part)
        value = value - part
    return parts


def page_kernel(q_ref, own_ref, other_ref, out_ref):
    core = own_ref[at_info:at_weight, :].astype(f32)[:, 3:4]
    pages = at_weight - at_info
    slots = out_ref.shape[0] * out_ref.shape[1]
    placed = jnp.zeros((slots, out_ref.shape[2]), f32)
    own = iota((QPK * pages, CH), 1) // PAGE == iota((QPK * pages, CH), 0) % pages
    lane = iota((pages, HD), 1)
    row_lane = iota((pages, q_ref.shape[0]), 1).astype(f32)
    slot_lane = iota((pages, slots), 1).astype(f32)
    for side, ref in enumerate((own_ref, other_ref)):
        info = ref[at_info:at_weight, :].astype(f32)
        group, request, earlier = info[:, 0:1], info[:, 1:2], info[:, 2:3]
        chip = jnp.floor(group * 0.5)
        mine = group - 2.0 * chip == core
        row = jnp.where(mine, chip * REQ + request, -1.0)
        slot = jnp.where(mine, chip * (2 * CAP) + side * CAP + earlier, -1.0)
        chosen = (row_lane == row).astype(f32).astype(bf16)
        placing = (slot_lane == slot).astype(f32).astype(bf16)
        asked = dot(chosen, q_ref[...], ((1,), (0,)))
        asked = [asked[:, h * HD : (h + 1) * HD] for h in range(QPK)]
        queries = jnp.concatenate(asked, axis=0).astype(bf16)
        scores = dot(queries, ref[:at_values, :], ((1,), (1,))) * scale
        scores = jnp.where(own, scores, neg_large)
        peak = jnp.max(scores, axis=1, keepdims=True)
        weights = jnp.where(own, jnp.exp(scores - peak), 0.0)
        total = jnp.sum(weights, axis=1, keepdims=True)
        values = dot(weights.astype(bf16), ref[at_values:at_info, :], ((1,), (0,))) / total
        extra = jnp.where(lane // ROWS == 5, request + 1.0, 0.0)
        parts = parts_of(peak, 3) + parts_of(total, 2)
        columns = []
        for h in range(QPK):
            part = slice(h * pages, (h + 1) * pages)
            columns.append(values[part])
            for block, column in enumerate(parts):
                extra = jnp.where(lane // REQ == block * QPK + h, column[part], extra)
        payload = jnp.concatenate(columns + [extra], axis=1).astype(bf16)
        placed = placed + dot(placing, payload, ((0,), (0,)))
    out_ref[...] = placed.reshape(out_ref.shape).astype(bf16)


def project_kernel(rows_ref, own_ref, other_ref, out_ref):
    first = own_ref[at_info : at_info + 16, :].astype(f32)[0:1, 3:4] == 0.0
    rows = rows_ref[...]
    own = dot(rows, own_ref[at_weight:, :], ((1,), (0,)))
    other = dot(rows, other_ref[at_weight:, :], ((1,), (0,)))
    out_ref[0] = jnp.where(first, own, other).astype(bf16)
    out_ref[1] = jnp.where(first, other, own).astype(bf16)


def combine_kernel(got_ref, sum_ref, peak_ref, total_ref, out_ref):
    slots = got_ref.shape[0]
    extra = got_ref[:, QPK * HD :].astype(f32)
    block = [extra] + [pltpu.roll(extra, HD - ROWS * i, 1) for i in range(1, 6)]
    lane = iota((slots, HD), 1)
    shown = (block[5] == (lane % REQ + 1).astype(f32)) & (lane < ROWS)
    peaks = jnp.where(shown, block[0] + block[1] + block[2], neg_large)
    totals = block[3] + block[4]
    eye = iota((ROWS, HD), 0) == iota((ROWS, HD), 1)
    home_peak = jnp.sum(jnp.where(eye, peak_ref[...], 0.0), axis=0, keepdims=True)
    home_total = jnp.sum(jnp.where(eye, total_ref[...], 0.0), axis=0, keepdims=True)
    top = jnp.maximum(jnp.max(peaks, axis=0, keepdims=True), home_peak)
    weights = jnp.where(shown, jnp.exp(peaks - top) * totals, 0.0)
    home = jnp.exp(home_peak - top)
    whole = jnp.sum(weights, axis=0, keepdims=True) + home * home_total
    whole = jnp.where(iota((1, HD), 1) < ROWS, whole, 1.0)
    low = (weights / whole).astype(bf16)[:, :ROWS]
    home_column = jnp.sum(jnp.where(eye, home / whole, 0.0), axis=1, keepdims=True)
    rows = sum_ref[...] * home_column
    head = iota((ROWS, HD), 0) // REQ
    for h in range(QPK):
        add = dot(low, got_ref[:, h * HD : (h + 1) * HD], ((0,), (0,)))
        rows = rows + jnp.where(head == h, add, 0.0)
    wide = jnp.concatenate([rows[h * REQ : (h + 1) * REQ, :] for h in range(QPK)], axis=1)
    out_ref[...] = jnp.broadcast_to(wide[None], out_ref.shape).astype(bf16)


def sum_kernel(terms_ref, out_ref):
    half = terms_ref.shape[0] // 2
    sums = []
    for c in range(2):
        total = terms_ref[c * half].astype(f32)
        for t in range(1, half):
            total = total + terms_ref[c * half + t].astype(f32)
        sums.append(total)
    blocks = []
    for x in range(terms_ref.shape[1] // REQ):
        blocks += [sums[c][x * REQ : (x + 1) * REQ] for c in range(2)]
    out_ref[...] = jnp.concatenate(blocks, axis=0).astype(bf16)


def on_device(
    prefill_q,
    prefill_k,
    prefill_v,
    span_offset,
    page_group,
    page_request,
    decode_q,
    cache_k,
    cache_v,
    cache_len,
    out_weight,
):
    chips = ("y", "x")
    peers = lax.axis_size(chips)
    width = decode_q.shape[1]

    asking, rows = call(
        repeat_kernel,
        (
            jax.ShapeDtypeStruct((peers,) + decode_q.shape, bf16),
            jax.ShapeDtypeStruct((ROWS, HD), bf16),
        ),
        decode_q,
    )
    asked = lax.all_to_all(asking, chips, split_axis=0, concat_axis=0, tiled=True)
    asked = asked.reshape(peers * REQ, width)

    core = lax.axis_index("c").reshape(1)
    small, ints = (page_group[:, 0], page_request, cache_len, span_offset, core), 0
    for piece, start in zip(small, (0, at_requests, at_lengths, at_offset, at_core)):
        ints = ints + jnp.pad(piece, (start, HD - start - piece.shape[0]))
    ints = ints.reshape(1, HD)
    own = call(
        pack_kernel,
        jax.ShapeDtypeStruct((at_end, HD), bf16),
        ints,
        prefill_k,
        prefill_v,
        out_weight,
        asking,
        unread=1,
    )
    other = lax.ppermute(own, "c", [(0, 1), (1, 0)])

    rows_of = jax.ShapeDtypeStruct((ROWS, HD), f32)
    home = call(
        resident_kernel,
        (rows_of,) * 3,
        rows,
        cache_k,
        cache_v,
        ints,
        flops=shadow_flops,
    )
    asked, other, home = lax.optimization_barrier((asked, other, home))
    sent = call(
        page_kernel,
        jax.ShapeDtypeStruct((peers, 2 * CAP, width + HD), bf16),
        asked,
        own,
        other,
    )
    got = lax.all_to_all(sent, chips, split_axis=0, concat_axis=0, tiled=True)
    got = got.reshape(peers * 2 * CAP, width + HD)

    repeated = call(
        combine_kernel, jax.ShapeDtypeStruct((peers, REQ, width), bf16), got, *home
    )
    everyone = lax.all_to_all(repeated, chips, split_axis=0, concat_axis=0, tiled=True)
    everyone = everyone.reshape(peers * REQ, width)
    shards = lax.axis_size("z")
    cores = lax.axis_size("c")
    terms = call(
        project_kernel,
        jax.ShapeDtypeStruct((cores, peers * REQ, HD), bf16),
        everyone,
        own,
        other,
    )
    terms = terms.reshape(cores * shards, peers * REQ // shards, HD)
    prefill_out = call(
        prefill_kernel,
        jax.ShapeDtypeStruct(prefill_q.shape, bf16),
        ints,
        prefill_q,
        own,
        terms,
        unread=1,
        flops=shadow_flops,
    )
    terms = lax.all_to_all(terms, ("c", "z"), split_axis=0, concat_axis=0, tiled=True)
    decode_out = call(
        sum_kernel, jax.ShapeDtypeStruct((peers * REQ * cores // shards, HD), bf16), terms
    )
    return (prefill_out, decode_out)


def solution(mesh):
    fine = Mesh(mesh.devices.reshape(8, 4, 2, 8), ("y", "x", "c", "z"))
    grp = ("y", "x", "c")
    in_specs = (
        P(grp, "z"),
        P(grp, "z"),
        P(grp, "z"),
        P(grp),
        P(grp, None),
        P(grp),
        P(grp, "z"),
        P(grp, None, "z"),
        P(grp, None, "z"),
        P(grp),
        P("z", grp),
    )
    out_specs = (P(grp, "z"), P("z", grp))
    return jax.shard_map(
        on_device, mesh=fine, in_specs=in_specs, out_specs=out_specs, check_vma=False
    )
```

```python
import math

import jax
import jax.numpy as jnp
from jax import lax
from jax.experimental import pallas as pl
from jax.experimental.pallas import tpu as pltpu
from jax.sharding import Mesh, PartitionSpec as P

HD = 128
QPK = 4
PAGE = 16
CAP = 2
REQ = 4
ROWS = QPK * REQ

rope_base = 500000.0
neg_large = -1e30
scale = 1.0 / math.sqrt(HD)
f32 = jnp.float32
bf16 = jnp.bfloat16
vmem_limit = 32 * 1024 * 1024
shadow_flops = 5 * 10**9
first_chip, first_shard = 18, 5
CH = 256
at_requests, at_lengths, at_offset, at_core = 16, 32, 32 + REQ, 33 + REQ
at_values, at_info, at_weight, at_end = CH, 2 * CH, 2 * CH + 16, 2 * CH + 16 + 512


def factors(offset):
    shape = (16, HD)
    lane, row = iota(shape, 1), iota(shape, 0)
    power = (lane % (HD // 2)).astype(f32) * (-2.0 / HD * math.log(rope_base))
    frequency = jnp.exp(power)
    sign = jnp.where(lane < HD // 2, -1.0, 1.0)

    def turn(position):
        angle_rad = position.astype(f32) * frequency
        return jnp.cos(angle_rad), jnp.sin(angle_rad) * sign

    fine, coarse = turn(row), turn(offset + 16 * row)
    cosine, sine_part = [], []
    for d in range(CH // 16):
        c, s = coarse[0][d : d + 1], coarse[1][d : d + 1]
        cosine.append(fine[0] * c - fine[1] * s)
        sine_part.append(fine[1] * c + fine[0] * s)
    return jnp.concatenate(cosine, axis=0), jnp.concatenate(sine_part, axis=0)


def dot(a, b, dims):
    return lax.dot_general(a, b, (dims, ((), ())), preferred_element_type=f32)


def exchange(blocks, axes, first):
    count = lax.axis_size(axes)
    seats = [[(seat + first) % count for seat in range(count)]]
    return lax.all_to_all(
        blocks, axes, split_axis=0, concat_axis=0, axis_index_groups=seats, tiled=True
    )


def iota(shape, axis):
    return lax.broadcasted_iota(jnp.int32, shape, axis)


def call(kernel, outs, *args, unread=0, flops=0):
    moved = sum(a.size * a.dtype.itemsize for a in (*args, *jax.tree.leaves(outs)))
    places = [pltpu.VMEM] * (len(args) - unread) + [pl.ANY] * unread
    return pl.pallas_call(
        kernel,
        out_shape=outs,
        in_specs=[pl.BlockSpec(memory_space=place) for place in places],
        cost_estimate=pl.CostEstimate(flops=flops, bytes_accessed=moved, transcendentals=0),
        compiler_params=pltpu.CompilerParams(vmem_limit_bytes=vmem_limit),
    )(*args)


def rotate(values, cosine, sine_part):
    values = values.astype(f32)
    return (values * cosine + pltpu.roll(values, HD // 2, 1) * sine_part).astype(bf16)


def pack_kernel(
    ints_ref, k_ref, v_ref, weight_ref, _, pack_ref
):
    pack_ref[:at_values, :] = rotate(k_ref[...], *factors(ints_ref[:, at_offset : at_offset + 1]))
    pack_ref[at_values:at_info, :] = v_ref[...]
    pack_ref[at_weight:, :] = weight_ref[...]

    pages = at_requests
    eye = iota((pages, pages), 0) == iota((pages, pages), 1)
    group_row = ints_ref[:, :pages].astype(f32)
    group = jnp.sum(jnp.where(eye, group_row, 0.0), axis=1, keepdims=True)
    request = jnp.sum(jnp.where(eye, ints_ref[:, at_requests:at_lengths].astype(f32), 0.0), axis=1, keepdims=True)
    before = iota((pages, pages), 1) < iota((pages, pages), 0)
    earlier = jnp.where(before & (group == group_row), 1.0, 0.0)
    earlier = jnp.sum(earlier, axis=1, keepdims=True)
    lane = iota((pages, HD), 1)
    core = ints_ref[:, at_core : at_core + 1].astype(f32)
    info = jnp.where(lane == 0, group, jnp.where(lane == 1, request, earlier))
    info = jnp.where(lane == 3, core, info)
    pack_ref[at_info:at_weight, :] = info.astype(bf16)


def prefill_kernel(ints_ref, q_ref, pack_ref, _, out_ref):
    cosine, sine_part = factors(ints_ref[:, at_offset : at_offset + 1])
    keys, values = pack_ref[:at_values, :], pack_ref[at_values:at_info, :]
    causal = iota((CH, CH), 1) <= iota((CH, CH), 0)
    for h in range(QPK):
        part = slice(h * HD, (h + 1) * HD)
        queries = rotate(q_ref[:, part], cosine, sine_part)
        scores = dot(queries, keys, ((1,), (1,))) * scale
        scores = jnp.where(causal, scores, neg_large)
        weights = jnp.exp(scores - jnp.max(scores, axis=1, keepdims=True))
        weights = weights * (1.0 / jnp.sum(weights, axis=1, keepdims=True))
        out_ref[:, part] = dot(weights.astype(bf16), values, ((1,), (0,))).astype(bf16)


def resident_kernel(rows_ref, k_ref, v_ref, ints_ref, sum_ref, peak_ref, total_ref):
    rows = rows_ref[...]
    slots = k_ref.shape[1]
    request = iota((ROWS, 1), 0) % REQ
    live = jnp.zeros((ROWS, 1), jnp.int32)
    scores = jnp.zeros((ROWS, slots), f32)
    for r in range(REQ):
        live = jnp.where(request == r, ints_ref[:, at_lengths + r : at_lengths + r + 1], live)
        scores = jnp.where(request == r, dot(rows, k_ref[r], ((1,), (1,))), scores)
    shown = iota((ROWS, slots), 1) < live
    scores = jnp.where(shown, scores * scale, neg_large)
    peak = jnp.max(scores, axis=1, keepdims=True)
    weights = jnp.where(shown, jnp.exp(scores - peak), 0.0)
    total = jnp.sum(weights, axis=1, keepdims=True)
    low = weights.astype(bf16)
    summed = jnp.zeros((ROWS, HD), f32)
    for r in range(REQ):
        summed = jnp.where(request == r, dot(low, v_ref[r], ((1,), (0,))), summed)
    sum_ref[...] = summed
    peak_ref[...] = jnp.broadcast_to(peak, (ROWS, HD))
    total_ref[...] = jnp.broadcast_to(total, (ROWS, HD))


def repeat_kernel(q_ref, out_ref, rows_ref):
    out_ref[...] = jnp.broadcast_to(q_ref[...][None], out_ref.shape)
    q = q_ref[...].astype(f32)
    rows = jnp.concatenate([q[:, h * HD : (h + 1) * HD] for h in range(QPK)], axis=0)
    rows_ref[...] = rows.astype(bf16)


def parts_of(value, count):
    parts = []
    for _ in range(count):
        part = value.astype(bf16).astype(f32)
        parts.append(part)
        value = value - part
    return parts


def page_kernel(q_ref, own_ref, other_ref, out_ref):
    pages = at_weight - at_info
    slots = out_ref.shape[0] * out_ref.shape[1]
    sides = (own_ref, other_ref)
    info = jnp.concatenate([ref[at_info:at_weight, :].astype(f32) for ref in sides], axis=0)
    group, request, earlier, core = info[:, 0:1], info[:, 1:2], info[:, 2:3], info[0:1, 3:4]
    chip = jnp.floor(group * 0.5)
    mine = group - 2.0 * chip == core
    both = iota((2 * pages, 1), 0)
    side = jnp.where(both < pages, 0.0, float(CAP))
    seat = chip - first_chip
    seat = jnp.where(seat < 0.0, seat + out_ref.shape[0], seat)
    row = jnp.where(mine, seat * REQ + request, -1.0)
    slot = jnp.where(mine, seat * (2 * CAP) + side + earlier, -1.0)
    chosen = (iota((2 * pages, q_ref.shape[0]), 1).astype(f32) == row).astype(f32).astype(bf16)
    placing = (iota((2 * pages, slots), 1).astype(f32) == slot).astype(f32).astype(bf16)
    asked = dot(chosen, q_ref[...], ((1,), (0,)))
    own = iota((QPK * pages, CH), 1) // PAGE == iota((QPK * pages, CH), 0) % pages
    wide_lane, wide_row = iota((QPK * pages, HD), 1), iota((QPK * pages, HD), 0)
    spot = jnp.where(wide_lane // REQ % QPK == wide_row // pages, wide_lane // ROWS, -1)
    lane = iota((pages, HD), 1)
    payload = []
    for i, ref in enumerate(sides):
        here = slice(i * pages, (i + 1) * pages)
        queries = [asked[here, h * HD : (h + 1) * HD] for h in range(QPK)]
        queries = jnp.concatenate(queries, axis=0).astype(bf16)
        scores = dot(queries, ref[:at_values, :], ((1,), (1,))) * scale
        scores = jnp.where(own, scores, neg_large)
        peak = jnp.max(scores, axis=1, keepdims=True)
        weights = jnp.where(own, jnp.exp(scores - peak), 0.0)
        total = jnp.sum(weights, axis=1, keepdims=True)
        values = dot(weights.astype(bf16), ref[at_values:at_info, :], ((1,), (0,))) / total
        wide = jnp.zeros((QPK * pages, HD), f32)
        for block, column in enumerate(parts_of(peak, 3) + parts_of(total, 2)):
            wide = jnp.where(spot == block, column, wide)
        extra = jnp.where(lane // ROWS == 5, request[here] + 1.0, 0.0)
        columns = []
        for h in range(QPK):
            part = slice(h * pages, (h + 1) * pages)
            columns.append(values[part])
            extra = extra + wide[part]
        payload.append(jnp.concatenate(columns + [extra], axis=1))
    payload = jnp.concatenate(payload, axis=0).astype(bf16)
    placed = dot(placing, payload, ((0,), (0,)))
    out_ref[...] = placed.reshape(out_ref.shape).astype(bf16)


def project_kernel(rows_ref, own_ref, other_ref, out_ref):
    first = own_ref[at_info : at_info + 16, :].astype(f32)[0:1, 3:4] == 0.0
    rows = rows_ref[...]
    start = rows.shape[0] - first_chip * REQ

    def product(weight):
        terms = dot(rows, weight, ((1,), (0,)))
        return jnp.concatenate([terms[start:], terms[:start]], axis=0)

    own, other = product(own_ref[at_weight:, :]), product(other_ref[at_weight:, :])
    blocks = jnp.where(first, own, other).astype(bf16), jnp.where(first, other, own).astype(bf16)
    count, height = out_ref.shape[0], out_ref.shape[1]
    for seat in range(count):
        c, z = divmod((seat + first_shard) % count, count // 2)
        out_ref[seat] = blocks[c][z * height : (z + 1) * height]


def combine_kernel(got_ref, sum_ref, peak_ref, total_ref, out_ref):
    slots = got_ref.shape[0]
    extra = got_ref[:, QPK * HD :].astype(f32)
    block = [extra] + [pltpu.roll(extra, HD - ROWS * i, 1) for i in range(1, 6)]
    lane = iota((slots, HD), 1)
    shown = (block[5] == (lane % REQ + 1).astype(f32)) & (lane < ROWS)
    peaks = jnp.where(shown, block[0] + block[1] + block[2], neg_large)
    totals = block[3] + block[4]
    eye = iota((ROWS, HD), 0) == iota((ROWS, HD), 1)
    home_peak = jnp.sum(jnp.where(eye, peak_ref[...], 0.0), axis=0, keepdims=True)
    home_total = jnp.sum(jnp.where(eye, total_ref[...], 0.0), axis=0, keepdims=True)
    top = jnp.maximum(jnp.max(peaks, axis=0, keepdims=True), home_peak)
    weights = jnp.where(shown, jnp.exp(peaks - top) * totals, 0.0)
    home = jnp.exp(home_peak - top)
    whole = jnp.sum(weights, axis=0, keepdims=True) + home * home_total
    whole = jnp.where(iota((1, HD), 1) < ROWS, whole, 1.0)
    low = (weights / whole).astype(bf16)[:, :ROWS]
    home_column = jnp.sum(jnp.where(eye, home / whole, 0.0), axis=1, keepdims=True)
    rows = sum_ref[...] * home_column
    head = iota((ROWS, HD), 0) // REQ
    for h in range(QPK):
        add = dot(low, got_ref[:, h * HD : (h + 1) * HD], ((0,), (0,)))
        rows = rows + jnp.where(head == h, add, 0.0)
    wide = jnp.concatenate([rows[h * REQ : (h + 1) * REQ, :] for h in range(QPK)], axis=1)
    out_ref[...] = jnp.broadcast_to(wide[None], out_ref.shape).astype(bf16)


def sum_kernel(terms_ref, out_ref):
    count = terms_ref.shape[0]
    half = count // 2
    sums = []
    for c in range(2):
        total = terms_ref[(c * half - first_shard) % count].astype(f32)
        for t in range(1, half):
            total = total + terms_ref[(c * half + t - first_shard) % count].astype(f32)
        sums.append(total)
    blocks = []
    for x in range(terms_ref.shape[1] // REQ):
        blocks += [sums[c][x * REQ : (x + 1) * REQ] for c in range(2)]
    out_ref[...] = jnp.concatenate(blocks, axis=0).astype(bf16)


def on_device(
    prefill_q,
    prefill_k,
    prefill_v,
    span_offset,
    page_group,
    page_request,
    decode_q,
    cache_k,
    cache_v,
    cache_len,
    out_weight,
):
    chips = ("y", "x")
    peers = lax.axis_size(chips)
    width = decode_q.shape[1]

    asking, rows = call(
        repeat_kernel,
        (
            jax.ShapeDtypeStruct((peers,) + decode_q.shape, bf16),
            jax.ShapeDtypeStruct((ROWS, HD), bf16),
        ),
        decode_q,
    )
    asked = exchange(asking, chips, first_chip)
    asked = asked.reshape(peers * REQ, width)

    core = lax.axis_index("c").reshape(1)
    small, ints = (page_group[:, 0], page_request, cache_len, span_offset, core), 0
    for piece, start in zip(small, (0, at_requests, at_lengths, at_offset, at_core)):
        ints = ints + jnp.pad(piece, (start, HD - start - piece.shape[0]))
    ints = ints.reshape(1, HD)
    own = call(
        pack_kernel,
        jax.ShapeDtypeStruct((at_end, HD), bf16),
        ints,
        prefill_k,
        prefill_v,
        out_weight,
        asking,
        unread=1,
    )
    other = lax.ppermute(own, "c", [(0, 1), (1, 0)])

    rows_of = jax.ShapeDtypeStruct((ROWS, HD), f32)
    home = call(
        resident_kernel,
        (rows_of,) * 3,
        rows,
        cache_k,
        cache_v,
        ints,
        flops=shadow_flops,
    )
    asked, other, home = lax.optimization_barrier((asked, other, home))
    sent = call(
        page_kernel,
        jax.ShapeDtypeStruct((peers, 2 * CAP, width + HD), bf16),
        asked,
        own,
        other,
    )
    got = exchange(sent, chips, first_chip)
    got = got.reshape(peers * 2 * CAP, width + HD)

    repeated = call(
        combine_kernel, jax.ShapeDtypeStruct((peers, REQ, width), bf16), got, *home
    )
    everyone = exchange(repeated, chips, first_chip)
    everyone = everyone.reshape(peers * REQ, width)
    shards = lax.axis_size("z")
    cores = lax.axis_size("c")
    terms = call(
        project_kernel,
        jax.ShapeDtypeStruct((cores * shards, peers * REQ // shards, HD), bf16),
        everyone,
        own,
        other,
    )
    prefill_out = call(
        prefill_kernel,
        jax.ShapeDtypeStruct(prefill_q.shape, bf16),
        ints,
        prefill_q,
        own,
        terms,
        unread=1,
        flops=shadow_flops,
    )
    terms = exchange(terms, ("c", "z"), first_shard)
    decode_out = call(
        sum_kernel, jax.ShapeDtypeStruct((peers * REQ * cores // shards, HD), bf16), terms
    )
    return (prefill_out, decode_out)


def solution(mesh):
    fine = Mesh(mesh.devices.reshape(8, 4, 2, 8), ("y", "x", "c", "z"))
    grp = ("y", "x", "c")
    in_specs = (
        P(grp, "z"),
        P(grp, "z"),
        P(grp, "z"),
        P(grp),
        P(grp, None),
        P(grp),
        P(grp, "z"),
        P(grp, None, "z"),
        P(grp, None, "z"),
        P(grp),
        P("z", grp),
    )
    out_specs = (P(grp, "z"), P("z", grp))
    return jax.shard_map(
        on_device, mesh=fine, in_specs=in_specs, out_specs=out_specs, check_vma=False
    )
```

```python
import math

import jax
import jax.numpy as jnp
from jax import lax
from jax.experimental import pallas as pl
from jax.experimental.pallas import tpu as pltpu
from jax.sharding import Mesh, PartitionSpec as P

HD = 128
QPK = 4
PAGE = 16
CAP = 2
REQ = 4
ROWS = QPK * REQ

rope_base = 500000.0
neg_large = -1e30
scale = 1.0 / math.sqrt(HD)
f32 = jnp.float32
bf16 = jnp.bfloat16
vmem_limit = 32 * 1024 * 1024
shadow_flops = 5 * 10**9
first_chip, first_shard = 18, 4
CH = 256
at_requests, at_lengths, at_offset, at_core = 16, 32, 32 + REQ, 33 + REQ
at_values, at_info, at_weight, at_end = CH, 2 * CH, 2 * CH + 16, 2 * CH + 16 + 512


def factors(offset):
    shape = (16, HD)
    lane, row = iota(shape, 1), iota(shape, 0)
    power = (lane % (HD // 2)).astype(f32) * (-2.0 / HD * math.log(rope_base))
    frequency = jnp.exp(power)
    sign = jnp.where(lane < HD // 2, -1.0, 1.0)

    def turn(position):
        angle_rad = position.astype(f32) * frequency
        return jnp.cos(angle_rad), jnp.sin(angle_rad) * sign

    fine, coarse = turn(row), turn(offset + 16 * row)
    cosine, sine_part = [], []
    for d in range(CH // 16):
        c, s = coarse[0][d : d + 1], coarse[1][d : d + 1]
        cosine.append(fine[0] * c - fine[1] * s)
        sine_part.append(fine[1] * c + fine[0] * s)
    return jnp.concatenate(cosine, axis=0), jnp.concatenate(sine_part, axis=0)


def dot(a, b, dims):
    return lax.dot_general(a, b, (dims, ((), ())), preferred_element_type=f32)


def exchange(blocks, axes, first):
    count = lax.axis_size(axes)
    seats = [[(seat + first) % count for seat in range(count)]]
    return lax.all_to_all(
        blocks, axes, split_axis=0, concat_axis=0, axis_index_groups=seats, tiled=True
    )


def iota(shape, axis):
    return lax.broadcasted_iota(jnp.int32, shape, axis)


def call(kernel, outs, *args, unread=0, flops=0):
    moved = sum(a.size * a.dtype.itemsize for a in (*args, *jax.tree.leaves(outs)))
    places = [pltpu.VMEM] * (len(args) - unread) + [pl.ANY] * unread
    return pl.pallas_call(
        kernel,
        out_shape=outs,
        in_specs=[pl.BlockSpec(memory_space=place) for place in places],
        cost_estimate=pl.CostEstimate(flops=flops, bytes_accessed=moved, transcendentals=0),
        compiler_params=pltpu.CompilerParams(vmem_limit_bytes=vmem_limit),
    )(*args)


def rotate(values, cosine, sine_part):
    values = values.astype(f32)
    return (values * cosine + pltpu.roll(values, HD // 2, 1) * sine_part).astype(bf16)


def pack_kernel(
    ints_ref, k_ref, v_ref, weight_ref, _, pack_ref
):
    pack_ref[:at_values, :] = rotate(k_ref[...], *factors(ints_ref[:, at_offset : at_offset + 1]))
    pack_ref[at_values:at_info, :] = v_ref[...]
    pack_ref[at_weight:, :] = weight_ref[...]

    pages = at_requests
    eye = iota((pages, pages), 0) == iota((pages, pages), 1)
    group_row = ints_ref[:, :pages].astype(f32)
    group = jnp.sum(jnp.where(eye, group_row, 0.0), axis=1, keepdims=True)
    request = jnp.sum(jnp.where(eye, ints_ref[:, at_requests:at_lengths].astype(f32), 0.0), axis=1, keepdims=True)
    before = iota((pages, pages), 1) < iota((pages, pages), 0)
    earlier = jnp.where(before & (group == group_row), 1.0, 0.0)
    earlier = jnp.sum(earlier, axis=1, keepdims=True)
    lane = iota((pages, HD), 1)
    core = ints_ref[:, at_core : at_core + 1].astype(f32)
    info = jnp.where(lane == 0, group, jnp.where(lane == 1, request, earlier))
    info = jnp.where(lane == 3, core, info)
    pack_ref[at_info:at_weight, :] = info.astype(bf16)


def prefill_kernel(ints_ref, q_ref, pack_ref, _, out_ref):
    cosine, sine_part = factors(ints_ref[:, at_offset : at_offset + 1])
    keys, values = pack_ref[:at_values, :], pack_ref[at_values:at_info, :]
    causal = iota((CH, CH), 1) <= iota((CH, CH), 0)
    for h in range(QPK):
        part = slice(h * HD, (h + 1) * HD)
        queries = rotate(q_ref[:, part], cosine, sine_part)
        scores = dot(queries, keys, ((1,), (1,))) * scale
        scores = jnp.where(causal, scores, neg_large)
        weights = jnp.exp(scores - jnp.max(scores, axis=1, keepdims=True))
        weights = weights * (1.0 / jnp.sum(weights, axis=1, keepdims=True))
        out_ref[:, part] = dot(weights.astype(bf16), values, ((1,), (0,))).astype(bf16)


def resident_kernel(rows_ref, k_ref, ints_ref, low_ref, peak_ref, total_ref):
    rows = rows_ref[...]
    slots = k_ref.shape[1]
    request = iota((ROWS, 1), 0) % REQ
    live = jnp.zeros((ROWS, 1), jnp.int32)
    scores = jnp.zeros((ROWS, slots), f32)
    for r in range(REQ):
        live = jnp.where(request == r, ints_ref[:, at_lengths + r : at_lengths + r + 1], live)
        scores = jnp.where(request == r, dot(rows, k_ref[r], ((1,), (1,))), scores)
    shown = iota((ROWS, slots), 1) < live
    scores = jnp.where(shown, scores * scale, neg_large)
    peak = jnp.max(scores, axis=1, keepdims=True)
    weights = jnp.where(shown, jnp.exp(scores - peak), 0.0)
    total = jnp.sum(weights, axis=1, keepdims=True)
    low_ref[...] = weights.astype(bf16)
    peak_ref[...] = jnp.broadcast_to(peak, (ROWS, HD))
    total_ref[...] = jnp.broadcast_to(total, (ROWS, HD))


def repeat_kernel(q_ref, out_ref, rows_ref):
    out_ref[...] = jnp.broadcast_to(q_ref[...][None], out_ref.shape)
    q = q_ref[...].astype(f32)
    rows = jnp.concatenate([q[:, h * HD : (h + 1) * HD] for h in range(QPK)], axis=0)
    rows_ref[...] = rows.astype(bf16)


def parts_of(value, count):
    parts = []
    for _ in range(count):
        part = value.astype(bf16).astype(f32)
        parts.append(part)
        value = value - part
    return parts


def page_kernel(q_ref, own_ref, other_ref, out_ref):
    pages = at_weight - at_info
    slots = out_ref.shape[0] * out_ref.shape[1]
    sides = (own_ref, other_ref)
    info = jnp.concatenate([ref[at_info:at_weight, :].astype(f32) for ref in sides], axis=0)
    group, request, earlier, core = info[:, 0:1], info[:, 1:2], info[:, 2:3], info[0:1, 3:4]
    chip = jnp.floor(group * 0.5)
    mine = group - 2.0 * chip == core
    both = iota((2 * pages, 1), 0)
    side = jnp.where(both < pages, 0.0, float(CAP))
    seat = chip - first_chip
    seat = jnp.where(seat < 0.0, seat + out_ref.shape[0], seat)
    row = jnp.where(mine, seat * REQ + request, -1.0)
    slot = jnp.where(mine, seat * (2 * CAP) + side + earlier, -1.0)
    chosen = (iota((2 * pages, q_ref.shape[0]), 1).astype(f32) == row).astype(f32).astype(bf16)
    placing = (iota((2 * pages, slots), 1).astype(f32) == slot).astype(f32).astype(bf16)
    asked = dot(chosen, q_ref[...], ((1,), (0,)))
    own = iota((QPK * pages, CH), 1) // PAGE == iota((QPK * pages, CH), 0) % pages
    wide_lane, wide_row = iota((QPK * pages, HD), 1), iota((QPK * pages, HD), 0)
    spot = jnp.where(wide_lane // REQ % QPK == wide_row // pages, wide_lane // ROWS, -1)
    lane = iota((pages, HD), 1)
    payload = []
    for i, ref in enumerate(sides):
        here = slice(i * pages, (i + 1) * pages)
        queries = [asked[here, h * HD : (h + 1) * HD] for h in range(QPK)]
        queries = jnp.concatenate(queries, axis=0).astype(bf16)
        scores = dot(queries, ref[:at_values, :], ((1,), (1,))) * scale
        scores = jnp.where(own, scores, neg_large)
        peak = jnp.max(scores, axis=1, keepdims=True)
        weights = jnp.where(own, jnp.exp(scores - peak), 0.0)
        total = jnp.sum(weights, axis=1, keepdims=True)
        values = dot(weights.astype(bf16), ref[at_values:at_info, :], ((1,), (0,))) / total
        wide = jnp.zeros((QPK * pages, HD), f32)
        for block, column in enumerate(parts_of(peak, 3) + parts_of(total, 2)):
            wide = jnp.where(spot == block, column, wide)
        extra = jnp.where(lane // ROWS == 5, request[here] + 1.0, 0.0)
        columns = []
        for h in range(QPK):
            part = slice(h * pages, (h + 1) * pages)
            columns.append(values[part])
            extra = extra + wide[part]
        payload.append(jnp.concatenate(columns + [extra], axis=1))
    payload = jnp.concatenate(payload, axis=0).astype(bf16)
    placed = dot(placing, payload, ((0,), (0,)))
    out_ref[...] = placed.reshape(out_ref.shape).astype(bf16)


def project_kernel(rows_ref, own_ref, other_ref, out_ref):
    first = own_ref[at_info : at_info + 16, :].astype(f32)[0:1, 3:4] == 0.0
    rows = rows_ref[...]
    start = rows.shape[0] - first_chip * REQ

    def product(weight):
        terms = dot(rows, weight, ((1,), (0,)))
        return jnp.concatenate([terms[start:], terms[:start]], axis=0)

    own, other = product(own_ref[at_weight:, :]), product(other_ref[at_weight:, :])
    blocks = jnp.where(first, own, other).astype(bf16), jnp.where(first, other, own).astype(bf16)
    count, height = out_ref.shape[0], out_ref.shape[1]
    for seat in range(count):
        c, z = divmod((seat + first_shard) % count, count // 2)
        out_ref[seat] = blocks[c][z * height : (z + 1) * height]


def combine_kernel(got_ref, low_ref, peak_ref, total_ref, v_ref, out_ref):
    slots = got_ref.shape[0]
    extra = got_ref[:, QPK * HD :].astype(f32)
    block = [extra] + [pltpu.roll(extra, HD - ROWS * i, 1) for i in range(1, 6)]
    lane = iota((slots, HD), 1)
    shown = (block[5] == (lane % REQ + 1).astype(f32)) & (lane < ROWS)
    peaks = jnp.where(shown, block[0] + block[1] + block[2], neg_large)
    totals = block[3] + block[4]
    eye = iota((ROWS, HD), 0) == iota((ROWS, HD), 1)
    home_peak = jnp.sum(jnp.where(eye, peak_ref[...], 0.0), axis=0, keepdims=True)
    home_total = jnp.sum(jnp.where(eye, total_ref[...], 0.0), axis=0, keepdims=True)
    top = jnp.maximum(jnp.max(peaks, axis=0, keepdims=True), home_peak)
    weights = jnp.where(shown, jnp.exp(peaks - top) * totals, 0.0)
    home = jnp.exp(home_peak - top)
    whole = jnp.sum(weights, axis=0, keepdims=True) + home * home_total
    whole = jnp.where(iota((1, HD), 1) < ROWS, whole, 1.0)
    low = (weights / whole).astype(bf16)[:, :ROWS]
    home_column = jnp.sum(jnp.where(eye, home / whole, 0.0), axis=1, keepdims=True)
    summed = jnp.zeros((ROWS, HD), f32)
    request = iota((ROWS, 1), 0) % REQ
    for r in range(REQ):
        add = dot(low_ref[...], v_ref[r], ((1,), (0,)))
        summed = jnp.where(request == r, add, summed)
    rows = summed * home_column
    head = iota((ROWS, HD), 0) // REQ
    for h in range(QPK):
        add = dot(low, got_ref[:, h * HD : (h + 1) * HD], ((0,), (0,)))
        rows = rows + jnp.where(head == h, add, 0.0)
    wide = jnp.concatenate([rows[h * REQ : (h + 1) * REQ, :] for h in range(QPK)], axis=1)
    out_ref[...] = jnp.broadcast_to(wide[None], out_ref.shape).astype(bf16)


def sum_kernel(terms_ref, out_ref):
    count = terms_ref.shape[0]
    half = count // 2
    sums = []
    for c in range(2):
        total = terms_ref[(c * half - first_shard) % count].astype(f32)
        for t in range(1, half):
            total = total + terms_ref[(c * half + t - first_shard) % count].astype(f32)
        sums.append(total)
    blocks = []
    for x in range(terms_ref.shape[1] // REQ):
        blocks += [sums[c][x * REQ : (x + 1) * REQ] for c in range(2)]
    out_ref[...] = jnp.concatenate(blocks, axis=0).astype(bf16)


def on_device(
    prefill_q,
    prefill_k,
    prefill_v,
    span_offset,
    page_group,
    page_request,
    decode_q,
    cache_k,
    cache_v,
    cache_len,
    out_weight,
):
    chips = ("y", "x")
    peers = lax.axis_size(chips)
    width = decode_q.shape[1]

    asking, rows = call(
        repeat_kernel,
        (
            jax.ShapeDtypeStruct((peers,) + decode_q.shape, bf16),
            jax.ShapeDtypeStruct((ROWS, HD), bf16),
        ),
        decode_q,
    )
    asked = exchange(asking, chips, first_chip)
    asked = asked.reshape(peers * REQ, width)

    core = lax.axis_index("c").reshape(1)
    small, ints = (page_group[:, 0], page_request, cache_len, span_offset, core), 0
    for piece, start in zip(small, (0, at_requests, at_lengths, at_offset, at_core)):
        ints = ints + jnp.pad(piece, (start, HD - start - piece.shape[0]))
    ints = ints.reshape(1, HD)
    own = call(
        pack_kernel,
        jax.ShapeDtypeStruct((at_end, HD), bf16),
        ints,
        prefill_k,
        prefill_v,
        out_weight,
        asking,
        unread=1,
    )
    other = lax.ppermute(own, "c", [(0, 1), (1, 0)])

    rows_of = jax.ShapeDtypeStruct((ROWS, HD), f32)
    home = call(
        resident_kernel,
        (jax.ShapeDtypeStruct((ROWS, cache_k.shape[1]), bf16), rows_of, rows_of),
        rows,
        cache_k,
        ints,
        flops=shadow_flops,
    )
    asked, other, home = lax.optimization_barrier((asked, other, home))
    sent = call(
        page_kernel,
        jax.ShapeDtypeStruct((peers, 2 * CAP, width + HD), bf16),
        asked,
        own,
        other,
    )
    got = exchange(sent, chips, first_chip)
    got = got.reshape(peers * 2 * CAP, width + HD)

    repeated = call(
        combine_kernel, jax.ShapeDtypeStruct((peers, REQ, width), bf16), got, *home, cache_v
    )
    everyone = exchange(repeated, chips, first_chip)
    everyone = everyone.reshape(peers * REQ, width)
    shards = lax.axis_size("z")
    cores = lax.axis_size("c")
    terms = call(
        project_kernel,
        jax.ShapeDtypeStruct((cores * shards, peers * REQ // shards, HD), bf16),
        everyone,
        own,
        other,
    )
    prefill_out = call(
        prefill_kernel,
        jax.ShapeDtypeStruct(prefill_q.shape, bf16),
        ints,
        prefill_q,
        own,
        terms,
        unread=1,
        flops=shadow_flops,
    )
    terms = exchange(terms, ("c", "z"), first_shard)
    decode_out = call(
        sum_kernel, jax.ShapeDtypeStruct((peers * REQ * cores // shards, HD), bf16), terms
    )
    return (prefill_out, decode_out)


def solution(mesh):
    fine = Mesh(mesh.devices.reshape(8, 4, 2, 8), ("y", "x", "c", "z"))
    grp = ("y", "x", "c")
    in_specs = (
        P(grp, "z"),
        P(grp, "z"),
        P(grp, "z"),
        P(grp),
        P(grp, None),
        P(grp),
        P(grp, "z"),
        P(grp, None, "z"),
        P(grp, None, "z"),
        P(grp),
        P("z", grp),
    )
    out_specs = (P(grp, "z"), P("z", grp))
    return jax.shard_map(
        on_device, mesh=fine, in_specs=in_specs, out_specs=out_specs, check_vma=False
    )
```

```python
import math

import jax
import jax.numpy as jnp
from jax import lax
from jax.experimental import pallas as pl
from jax.experimental.pallas import tpu as pltpu
from jax.sharding import Mesh, PartitionSpec as P

HD = 128
QPK = 4
PAGE = 16
CAP = 2
REQ = 4
ROWS = QPK * REQ

rope_base = 500000.0
neg_large = -1e30
scale = 1.0 / math.sqrt(HD)
f32 = jnp.float32
bf16 = jnp.bfloat16
vmem_limit = 32 * 1024 * 1024
shadow_flops = 5 * 10**9
first_chip, first_shard = 18, 12
CH = 256
at_requests, at_lengths, at_offset, at_core = 16, 32, 32 + REQ, 33 + REQ
at_values, at_info, at_weight, at_end = CH, 2 * CH, 2 * CH + 16, 2 * CH + 16 + 512


def factors(offset):
    shape = (16, HD)
    lane, row = iota(shape, 1), iota(shape, 0)
    power = (lane % (HD // 2)).astype(f32) * (-2.0 / HD * math.log(rope_base))
    frequency = jnp.exp(power)
    sign = jnp.where(lane < HD // 2, -1.0, 1.0)

    def turn(position):
        angle_rad = position.astype(f32) * frequency
        return jnp.cos(angle_rad), jnp.sin(angle_rad) * sign

    fine, coarse = turn(row), turn(offset + 16 * row)
    cosine, sine_part = [], []
    for d in range(CH // 16):
        c, s = coarse[0][d : d + 1], coarse[1][d : d + 1]
        cosine.append(fine[0] * c - fine[1] * s)
        sine_part.append(fine[1] * c + fine[0] * s)
    return jnp.concatenate(cosine, axis=0), jnp.concatenate(sine_part, axis=0)


def dot(a, b, dims):
    return lax.dot_general(a, b, (dims, ((), ())), preferred_element_type=f32)


def exchange(blocks, axes, first):
    count = lax.axis_size(axes)
    seats = [[(seat + first) % count for seat in range(count)]]
    return lax.all_to_all(
        blocks, axes, split_axis=0, concat_axis=0, axis_index_groups=seats, tiled=True
    )


def iota(shape, axis):
    return lax.broadcasted_iota(jnp.int32, shape, axis)


def call(kernel, outs, *args, unread=0, flops=0):
    moved = sum(a.size * a.dtype.itemsize for a in (*args, *jax.tree.leaves(outs)))
    places = [pltpu.VMEM] * (len(args) - unread) + [pl.ANY] * unread
    return pl.pallas_call(
        kernel,
        out_shape=outs,
        in_specs=[pl.BlockSpec(memory_space=place) for place in places],
        cost_estimate=pl.CostEstimate(flops=flops, bytes_accessed=moved, transcendentals=0),
        compiler_params=pltpu.CompilerParams(vmem_limit_bytes=vmem_limit),
    )(*args)


def rotate(values, cosine, sine_part):
    values = values.astype(f32)
    return (values * cosine + pltpu.roll(values, HD // 2, 1) * sine_part).astype(bf16)


def pack_kernel(
    ints_ref, k_ref, v_ref, weight_ref, _, pack_ref
):
    pack_ref[:at_values, :] = rotate(k_ref[...], *factors(ints_ref[:, at_offset : at_offset + 1]))
    pack_ref[at_values:at_info, :] = v_ref[...]
    pack_ref[at_weight:, :] = weight_ref[...]

    pages = at_requests
    eye = iota((pages, pages), 0) == iota((pages, pages), 1)
    group_row = ints_ref[:, :pages].astype(f32)
    group = jnp.sum(jnp.where(eye, group_row, 0.0), axis=1, keepdims=True)
    request = jnp.sum(jnp.where(eye, ints_ref[:, at_requests:at_lengths].astype(f32), 0.0), axis=1, keepdims=True)
    before = iota((pages, pages), 1) < iota((pages, pages), 0)
    earlier = jnp.where(before & (group == group_row), 1.0, 0.0)
    earlier = jnp.sum(earlier, axis=1, keepdims=True)
    lane = iota((pages, HD), 1)
    core = ints_ref[:, at_core : at_core + 1].astype(f32)
    info = jnp.where(lane == 0, group, jnp.where(lane == 1, request, earlier))
    info = jnp.where(lane == 3, core, info)
    pack_ref[at_info:at_weight, :] = info.astype(bf16)


def prefill_kernel(ints_ref, q_ref, pack_ref, _, out_ref):
    cosine, sine_part = factors(ints_ref[:, at_offset : at_offset + 1])
    keys, values = pack_ref[:at_values, :], pack_ref[at_values:at_info, :]
    causal = iota((CH, CH), 1) <= iota((CH, CH), 0)
    for h in range(QPK):
        part = slice(h * HD, (h + 1) * HD)
        queries = rotate(q_ref[:, part], cosine, sine_part)
        scores = dot(queries, keys, ((1,), (1,))) * scale
        scores = jnp.where(causal, scores, neg_large)
        weights = jnp.exp(scores - jnp.max(scores, axis=1, keepdims=True))
        weights = weights * (1.0 / jnp.sum(weights, axis=1, keepdims=True))
        out_ref[:, part] = dot(weights.astype(bf16), values, ((1,), (0,))).astype(bf16)


def resident_kernel(rows_ref, k_ref, ints_ref, low_ref, peak_ref, total_ref):
    rows = rows_ref[...]
    slots = k_ref.shape[1]
    request = iota((ROWS, 1), 0) % REQ
    live = jnp.zeros((ROWS, 1), jnp.int32)
    scores = jnp.zeros((ROWS, slots), f32)
    for r in range(REQ):
        live = jnp.where(request == r, ints_ref[:, at_lengths + r : at_lengths + r + 1], live)
        scores = jnp.where(request == r, dot(rows, k_ref[r], ((1,), (1,))), scores)
    shown = iota((ROWS, slots), 1) < live
    scores = jnp.where(shown, scores * scale, neg_large)
    peak = jnp.max(scores, axis=1, keepdims=True)
    weights = jnp.where(shown, jnp.exp(scores - peak), 0.0)
    total = jnp.sum(weights, axis=1, keepdims=True)
    low_ref[...] = weights.astype(bf16)
    peak_ref[...] = jnp.broadcast_to(peak, (ROWS, HD))
    total_ref[...] = jnp.broadcast_to(total, (ROWS, HD))


def repeat_kernel(q_ref, out_ref, rows_ref):
    out_ref[...] = jnp.broadcast_to(q_ref[...][None], out_ref.shape)
    q = q_ref[...].astype(f32)
    rows = jnp.concatenate([q[:, h * HD : (h + 1) * HD] for h in range(QPK)], axis=0)
    rows_ref[...] = rows.astype(bf16)


def parts_of(value, count):
    parts = []
    for _ in range(count):
        part = value.astype(bf16).astype(f32)
        parts.append(part)
        value = value - part
    return parts


def page_kernel(q_ref, own_ref, other_ref, out_ref):
    pages = at_weight - at_info
    slots = out_ref.shape[0] * out_ref.shape[1]
    sides = (own_ref, other_ref)
    info = jnp.concatenate([ref[at_info:at_weight, :].astype(f32) for ref in sides], axis=0)
    group, request, earlier, core = info[:, 0:1], info[:, 1:2], info[:, 2:3], info[0:1, 3:4]
    chip = jnp.floor(group * 0.5)
    mine = group - 2.0 * chip == core
    both = iota((2 * pages, 1), 0)
    side = jnp.where(both < pages, 0.0, float(CAP))
    seat = chip - first_chip
    seat = jnp.where(seat < 0.0, seat + out_ref.shape[0], seat)
    row = jnp.where(mine, seat * REQ + request, -1.0)
    slot = jnp.where(mine, seat * (2 * CAP) + side + earlier, -1.0)
    chosen = (iota((2 * pages, q_ref.shape[0]), 1).astype(f32) == row).astype(f32).astype(bf16)
    placing = (iota((2 * pages, slots), 1).astype(f32) == slot).astype(f32).astype(bf16)
    asked = dot(chosen, q_ref[...], ((1,), (0,)))
    own = iota((QPK * pages, CH), 1) // PAGE == iota((QPK * pages, CH), 0) % pages
    wide_lane, wide_row = iota((QPK * pages, HD), 1), iota((QPK * pages, HD), 0)
    spot = jnp.where(wide_lane // REQ % QPK == wide_row // pages, wide_lane // ROWS, -1)
    lane = iota((pages, HD), 1)
    payload = []
    for i, ref in enumerate(sides):
        here = slice(i * pages, (i + 1) * pages)
        queries = [asked[here, h * HD : (h + 1) * HD] for h in range(QPK)]
        queries = jnp.concatenate(queries, axis=0).astype(bf16)
        scores = dot(queries, ref[:at_values, :], ((1,), (1,))) * scale
        scores = jnp.where(own, scores, neg_large)
        peak = jnp.max(scores, axis=1, keepdims=True)
        weights = jnp.where(own, jnp.exp(scores - peak), 0.0)
        total = jnp.sum(weights, axis=1, keepdims=True)
        values = dot(weights.astype(bf16), ref[at_values:at_info, :], ((1,), (0,))) / total
        wide = jnp.zeros((QPK * pages, HD), f32)
        for block, column in enumerate(parts_of(peak, 3) + parts_of(total, 2)):
            wide = jnp.where(spot == block, column, wide)
        extra = jnp.where(lane // ROWS == 5, request[here] + 1.0, 0.0)
        columns = []
        for h in range(QPK):
            part = slice(h * pages, (h + 1) * pages)
            columns.append(values[part])
            extra = extra + wide[part]
        payload.append(jnp.concatenate(columns + [extra], axis=1))
    payload = jnp.concatenate(payload, axis=0).astype(bf16)
    placed = dot(placing, payload, ((0,), (0,)))
    out_ref[...] = placed.reshape(out_ref.shape).astype(bf16)


def project_kernel(rows_ref, own_ref, other_ref, out_ref):
    first = own_ref[at_info : at_info + 16, :].astype(f32)[0:1, 3:4] == 0.0
    rows = rows_ref[...]
    start = rows.shape[0] - first_chip * REQ

    def product(weight):
        terms = dot(rows, weight, ((1,), (0,)))
        return jnp.concatenate([terms[start:], terms[:start]], axis=0)

    own, other = product(own_ref[at_weight:, :]), product(other_ref[at_weight:, :])
    blocks = jnp.where(first, own, other).astype(bf16), jnp.where(first, other, own).astype(bf16)
    count, height = out_ref.shape[0], out_ref.shape[1]
    for seat in range(count):
        c, z = divmod((seat + first_shard) % count, count // 2)
        out_ref[seat] = blocks[c][z * height : (z + 1) * height]


def combine_kernel(got_ref, low_ref, peak_ref, total_ref, v_ref, out_ref):
    slots = got_ref.shape[0]
    extra = got_ref[:, QPK * HD :].astype(f32)
    block = [extra] + [pltpu.roll(extra, HD - ROWS * i, 1) for i in range(1, 6)]
    lane = iota((slots, HD), 1)
    shown = (block[5] == (lane % REQ + 1).astype(f32)) & (lane < ROWS)
    peaks = jnp.where(shown, block[0] + block[1] + block[2], neg_large)
    totals = block[3] + block[4]
    eye = iota((ROWS, HD), 0) == iota((ROWS, HD), 1)
    home_peak = jnp.sum(jnp.where(eye, peak_ref[...], 0.0), axis=0, keepdims=True)
    home_total = jnp.sum(jnp.where(eye, total_ref[...], 0.0), axis=0, keepdims=True)
    top = jnp.maximum(jnp.max(peaks, axis=0, keepdims=True), home_peak)
    weights = jnp.where(shown, jnp.exp(peaks - top) * totals, 0.0)
    home = jnp.exp(home_peak - top)
    whole = jnp.sum(weights, axis=0, keepdims=True) + home * home_total
    whole = jnp.where(iota((1, HD), 1) < ROWS, whole, 1.0)
    low = (weights / whole).astype(bf16)[:, :ROWS]
    home_column = jnp.sum(jnp.where(eye, home / whole, 0.0), axis=1, keepdims=True)
    summed = jnp.zeros((ROWS, HD), f32)
    request = iota((ROWS, 1), 0) % REQ
    for r in range(REQ):
        add = dot(low_ref[...], v_ref[r], ((1,), (0,)))
        summed = jnp.where(request == r, add, summed)
    rows = summed * home_column
    head = iota((ROWS, HD), 0) // REQ
    for h in range(QPK):
        add = dot(low, got_ref[:, h * HD : (h + 1) * HD], ((0,), (0,)))
        rows = rows + jnp.where(head == h, add, 0.0)
    wide = jnp.concatenate([rows[h * REQ : (h + 1) * REQ, :] for h in range(QPK)], axis=1)
    out_ref[...] = jnp.broadcast_to(wide[None], out_ref.shape).astype(bf16)


def sum_kernel(terms_ref, out_ref):
    count = terms_ref.shape[0]
    half = count // 2
    sums = []
    for c in range(2):
        total = terms_ref[(c * half - first_shard) % count].astype(f32)
        for t in range(1, half):
            total = total + terms_ref[(c * half + t - first_shard) % count].astype(f32)
        sums.append(total)
    blocks = []
    for x in range(terms_ref.shape[1] // REQ):
        blocks += [sums[c][x * REQ : (x + 1) * REQ] for c in range(2)]
    out_ref[...] = jnp.concatenate(blocks, axis=0).astype(bf16)


def on_device(
    prefill_q,
    prefill_k,
    prefill_v,
    span_offset,
    page_group,
    page_request,
    decode_q,
    cache_k,
    cache_v,
    cache_len,
    out_weight,
):
    chips = ("y", "x")
    peers = lax.axis_size(chips)
    width = decode_q.shape[1]

    asking, rows = call(
        repeat_kernel,
        (
            jax.ShapeDtypeStruct((peers,) + decode_q.shape, bf16),
            jax.ShapeDtypeStruct((ROWS, HD), bf16),
        ),
        decode_q,
    )
    asked = exchange(asking, chips, first_chip)
    asked = asked.reshape(peers * REQ, width)

    core = lax.axis_index("c").reshape(1)
    small, ints = (page_group[:, 0], page_request, cache_len, span_offset, core), 0
    for piece, start in zip(small, (0, at_requests, at_lengths, at_offset, at_core)):
        ints = ints + jnp.pad(piece, (start, HD - start - piece.shape[0]))
    ints = ints.reshape(1, HD)
    own = call(
        pack_kernel,
        jax.ShapeDtypeStruct((at_end, HD), bf16),
        ints,
        prefill_k,
        prefill_v,
        out_weight,
        asking,
        unread=1,
    )
    other = lax.ppermute(own, "c", [(0, 1), (1, 0)])

    rows_of = jax.ShapeDtypeStruct((ROWS, HD), f32)
    home = call(
        resident_kernel,
        (jax.ShapeDtypeStruct((ROWS, cache_k.shape[1]), bf16), rows_of, rows_of),
        rows,
        cache_k,
        ints,
        flops=shadow_flops,
    )
    asked, other, home = lax.optimization_barrier((asked, other, home))
    sent = call(
        page_kernel,
        jax.ShapeDtypeStruct((peers, 2 * CAP, width + HD), bf16),
        asked,
        own,
        other,
    )
    got = exchange(sent, chips, first_chip)
    got = got.reshape(peers * 2 * CAP, width + HD)

    repeated = call(
        combine_kernel, jax.ShapeDtypeStruct((peers, REQ, width), bf16), got, *home, cache_v
    )
    everyone = exchange(repeated, chips, first_chip)
    everyone = everyone.reshape(peers * REQ, width)
    shards = lax.axis_size("z")
    cores = lax.axis_size("c")
    terms = call(
        project_kernel,
        jax.ShapeDtypeStruct((cores * shards, peers * REQ // shards, HD), bf16),
        everyone,
        own,
        other,
    )
    prefill_out = call(
        prefill_kernel,
        jax.ShapeDtypeStruct(prefill_q.shape, bf16),
        ints,
        prefill_q,
        own,
        terms,
        unread=1,
        flops=shadow_flops,
    )
    terms = exchange(terms, ("c", "z"), first_shard)
    decode_out = call(
        sum_kernel, jax.ShapeDtypeStruct((peers * REQ * cores // shards, HD), bf16), terms
    )
    return (prefill_out, decode_out)


def solution(mesh):
    fine = Mesh(mesh.devices.reshape(8, 4, 2, 8), ("y", "x", "c", "z"))
    grp = ("y", "x", "c")
    in_specs = (
        P(grp, "z"),
        P(grp, "z"),
        P(grp, "z"),
        P(grp),
        P(grp, None),
        P(grp),
        P(grp, "z"),
        P(grp, None, "z"),
        P(grp, None, "z"),
        P(grp),
        P("z", grp),
    )
    out_specs = (P(grp, "z"), P("z", grp))
    return jax.shard_map(
        on_device, mesh=fine, in_specs=in_specs, out_specs=out_specs, check_vma=False
    )
```
